32 devices in a mesh: ctx: 8 (over z, x), fft: 4 (over y, core).
Axes of the slice: x: 2, y: 2, z: 4, core: 2. Of those that a mesh axis runs over, the one named last changes fastest.
Arguments:
- tokens: bfloat16 [4096, 2048], P('ctx'), may hold values from -6 to 6
- w_in: bfloat16 [2048, 3, 2048], P(None, None, 'fft'), may hold values from -0.125 to 0.125
- short_taps: float32 [7, 384], replicated, may hold values from -2 to 2
- long_filter: float32 [4096, 128], P('ctx'), may hold values from -0.09375 to 0.09375
- skip_gain: float32 [2048], replicated, may hold values from -4 to 4
- w_out: bfloat16 [2048, 2048], P('fft'), may hold values from -0.125 to 0.125
Outputs:
- mixed: bfloat16 [4096, 2048], P(('ctx', 'fft'))
The draws below stay inside these ranges and needn't reach their ends.
All inputs are finite; a program needn't handle non-finite values.
Results may differ from the reference program's by a relative error of at most 0.014.
Values may be sent and summed in bfloat16 or wider, within the bound.
No kernel may reach another device: no remote copies, remote signals or barrier semaphores. Data moves between devices by JAX's collectives and lax.ppermute only.
A program may use at most 128 MiB of HBM per device.

```python
import jax
import jax.numpy as jnp
from jax import lax

D = 2048
GROUPS = 128
GS = 16
TAPS = 7
SEQ = 4096


def steps_of(own_key, extent, cuts, low, high):
    level = 1.0
    for axis_at, parts in cuts:
        steps = jax.random.uniform(jax.random.fold_in(jax.random.fold_in(own_key, 6), axis_at), (parts,), jnp.float32, low / len(cuts), high / len(cuts))
        level = level * jnp.repeat(jnp.exp(steps), extent[axis_at] // parts).reshape((-1,) + (1,) * (len(extent) - 1 - axis_at))
    return level


def scatter_about(stream_key, dims, spread, limit, shards=(), held_as=jnp.bfloat16):
    factor_of = steps_of(stream_key, dims, shards, -0.22, 0.18) if shards else 1.0
    drawn = jax.random.normal(stream_key, dims, jnp.float32) * spread * factor_of
    return jnp.minimum(jnp.maximum(drawn, -limit), limit).astype(held_as)


def setup_inputs(seed: int = 0) -> dict:
    keys = jax.random.split(jax.random.key(seed), 7)
    return {
        "tokens": scatter_about(keys[0], (SEQ, D), 1.0, 6.0, ((0, 8),)),
        "w_in": scatter_about(keys[1], (D, 3, D), D ** -0.5, 0.125, ((2, 4),)),
        "short_taps": scatter_about(keys[2], (TAPS, 3 * GROUPS), TAPS ** -0.5, 2.0, (), jnp.float32),
        "long_filter": scatter_about(keys[3], (SEQ, GROUPS), SEQ ** -0.5, 0.09375, ((0, 8),), jnp.float32),
        "skip_gain": scatter_about(keys[4], (D,), 1.0, 4.0, (), jnp.float32),
        "w_out": scatter_about(keys[5], (D, D), D ** -0.5, 0.125, ((0, 4),)),
    }


def reference(tokens, w_in, short_taps, long_filter, skip_gain, w_out):
    proj = jnp.dot(tokens, w_in.reshape(D, 3 * D), preferred_element_type=jnp.float32).astype(jnp.bfloat16)
    taps_full = jnp.repeat(short_taps, GS, axis=1)
    widened = proj.astype(jnp.float32)
    padded = jnp.concatenate([jnp.zeros((TAPS - 1, 3 * D), jnp.float32), widened], axis=0)
    feat = jnp.zeros_like(widened)
    for shift_count in range(TAPS):
        start = TAPS - 1 - shift_count
        feat = feat + taps_full[shift_count] * padded[start:start + SEQ]
    feat = feat.astype(jnp.bfloat16)
    query = feat[:, :D].astype(jnp.float32)
    mixed_in = feat[:, D:2 * D].astype(jnp.float32) * feat[:, 2 * D:].astype(jnp.float32)

    def per_group(group):
        filt = lax.dynamic_slice_in_dim(long_filter, group, 1, 1)[:, 0]
        block = lax.dynamic_slice_in_dim(mixed_in, group * GS, GS, 1)
        spectrum = jnp.fft.rfft(block, n=2 * SEQ, axis=0) * jnp.fft.rfft(filt, n=2 * SEQ)[:, None]
        return jnp.fft.irfft(spectrum, n=2 * SEQ, axis=0)[:SEQ].astype(jnp.float32)

    conv = lax.map(per_group, jnp.arange(GROUPS, dtype=jnp.int32))
    conv = conv.transpose(1, 0, 2).reshape(SEQ, D)
    gated = (query * (conv + skip_gain * mixed_in)).astype(jnp.bfloat16)
    return jnp.dot(gated, w_out, preferred_element_type=jnp.float32).astype(jnp.bfloat16)
```

```python
import functools

import jax
import jax.numpy as jnp
from jax import lax
from jax.experimental import pallas as pl
from jax.experimental.pallas import tpu as pltpu
from jax.sharding import PartitionSpec as P

MIB = 1 << 20
LANES = 128
RIM = 16
LAG = 256


def passed_along(block, axis, distance):
    devices = range(lax.axis_size(axis))
    route = [(i - distance, i) for i in devices if i - distance in devices]
    return lax.ppermute(block, axis, route)


def swapped(block, mask):
    return lax.ppermute(block, "fft", [(i, i ^ mask) for i in range(lax.axis_size("fft"))])


def project_kernel(streams, group_size, parts, rim, tokens, taps, weights, out, ext, wbuf, proj, coefs, sems):
    n_tok = tokens.shape[0]
    width = wbuf.shape[3]
    n_blocks = wbuf.shape[1]
    n_taps = taps.shape[1]
    first = pltpu.make_async_copy(rim, ext.at[pl.ds(0, RIM)], sems.at[0])
    main = pltpu.make_async_copy(tokens, ext.at[pl.ds(RIM, n_tok)], sems.at[1])
    first.start()
    main.start()
    loads = {}
    for blk in range(n_blocks):
        for k, stream in enumerate(streams):
            copy = pltpu.make_async_copy(
                weights.at[stream, :, pl.ds(blk * width, width)], wbuf.at[k, blk], sems.at[2 + blk * len(streams) + k]
            )
            copy.start()
            loads[blk, k] = copy
    n_groups = taps.shape[2]
    n_chan = n_groups * group_size
    spread = (
        lax.broadcasted_iota(jnp.int32, (n_groups, n_chan), 0)
        == lax.broadcasted_iota(jnp.int32, (n_groups, n_chan), 1) // group_size
    ).astype(jnp.float32)
    for k, stream in enumerate(streams):
        coefs[k] = jnp.dot(
            taps[stream], spread, precision=lax.Precision.HIGHEST, preferred_element_type=jnp.float32
        )
    first.wait()
    main.wait()
    chunk = min(128, n_tok)
    for blk in range(n_blocks):
        for k in range(len(streams)):
            loads[blk, k].wait()
            full = jnp.dot(ext[...], wbuf[k, blk], preferred_element_type=jnp.float32)
            full = full.astype(jnp.bfloat16).astype(jnp.float32)
            for tile in range(width // LANES):
                proj[k, tile] = full[:, tile * LANES : (tile + 1) * LANES]
        for tile in range(width // LANES):
            chan = blk * width + tile * LANES
            for row in range(0, n_tok, chunk):
                made = None
                for k in range(len(streams)):
                    feat = None
                    for j in range(n_taps):
                        term = coefs[k, j : j + 1, chan : chan + LANES] * proj[k, tile, pl.ds(RIM + row - j, chunk), :]
                        feat = term if feat is None else feat + term
                    feat = feat.astype(jnp.bfloat16).astype(jnp.float32)
                    made = feat if made is None else made * feat
                turned = made.T.astype(jnp.bfloat16)
                if parts == 1:
                    out[chan : chan + LANES, row : row + chunk] = turned
                else:
                    span = n_tok // parts
                    for at in range(0, chunk, span):
                        out[(row + at) // span, chan : chan + LANES, :] = turned[:, at : at + span]


def project(streams, group_size, parts, rim, tokens, taps, weights):
    n_tok, depth = tokens.shape
    block = weights.shape[2]
    width = min(256, block)
    n_streams = len(streams)
    shape = (block, n_tok) if parts == 1 else (parts, block, n_tok // parts)
    any_spec = pl.BlockSpec(memory_space=pl.ANY)
    vmem = pl.BlockSpec(memory_space=pltpu.VMEM)
    flops = 2 * n_tok * depth * block * n_streams
    return pl.pallas_call(
        functools.partial(project_kernel, streams, group_size, parts),
        out_shape=jax.ShapeDtypeStruct(shape, jnp.bfloat16),
        in_specs=[any_spec, any_spec, vmem, any_spec],
        out_specs=vmem,
        scratch_shapes=[
            pltpu.VMEM((RIM + n_tok, depth), jnp.bfloat16),
            pltpu.VMEM((n_streams, block // width, depth, width), jnp.bfloat16),
            pltpu.VMEM((n_streams, width // LANES, RIM + n_tok, LANES), jnp.float32),
            pltpu.VMEM((n_streams, taps.shape[1], block), jnp.float32),
            pltpu.SemaphoreType.DMA((2 + n_streams * (block // width),)),
        ],
        compiler_params=pltpu.CompilerParams(vmem_limit_bytes=24 * MIB),
        cost_estimate=pl.CostEstimate(
            flops=flops, bytes_accessed=2 * (n_tok * depth + depth * block * n_streams), transcendentals=0
        ),
    )(rim, tokens, taps, weights)


def lags_kernel(filt, out):
    n_src, n_groups, cols = filt.shape
    length = n_src * cols
    zeros = jnp.zeros((1, LANES), jnp.float32)
    for g in range(n_groups):
        row = [zeros] + [filt[s, g : g + 1, :].astype(jnp.float32) for s in range(n_src)] + [zeros]
        row = jnp.concatenate(row, axis=1)
        wide = jnp.broadcast_to(row, (LANES, length + 2 * LANES))
        turned = pltpu.roll(wide, 0, 1, stride=1, stride_axis=0)
        out[g] = turned[:, : length + LANES].astype(jnp.bfloat16)


def lag_table(filt):
    n_src, n_groups, cols = filt.shape
    length = n_src * cols
    return pl.pallas_call(
        lags_kernel,
        out_shape=jax.ShapeDtypeStruct((n_groups, LANES, length + LANES), jnp.bfloat16),
        in_specs=[pl.BlockSpec(memory_space=pltpu.VMEM)],
        out_specs=pl.BlockSpec(memory_space=pltpu.VMEM),
        compiler_params=pltpu.CompilerParams(vmem_limit_bytes=40 * MIB),
        cost_estimate=pl.CostEstimate(
            flops=4 * n_groups * LANES * length, bytes_accessed=2 * n_groups * LANES * length, transcendentals=0
        ),
    )(filt)


def convolve_kernel(span, rows, mixed, lags, gain, out, held, total):
    n_src, n_chan, cols = mixed.shape
    n_blocks = n_src * cols // LAG
    per_src = cols // LAG
    n_fft, n_ctx, _, piece = out.shape
    pieces = LAG // piece
    size = n_blocks * rows
    static = n_blocks <= 16
    lead = 0 if static else size

    def lag_block(g, d):
        if static:
            at = d * LAG
            return jnp.concatenate([lags[g, :, at + LANES : at + LANES + LAG], lags[g, :, at : at + LAG]], axis=0)
        at = pl.multiple_of(d * LAG, LAG)
        near = lags[g, :, pl.ds(pl.multiple_of(at + LANES, LANES), LAG)]
        return jnp.concatenate([near, lags[g, :, pl.ds(at, LAG)]], axis=0)

    for g in range(n_chan // span):
        chans = slice(g * span, (g + 1) * span)
        if rows != span or lead:
            held[...] = jnp.zeros_like(held)
        for i in range(n_blocks):
            block = mixed[i // per_src, chans, (i % per_src) * LAG : (i % per_src + 1) * LAG]
            held[lead + i * rows : lead + i * rows + span, :] = block
        if static:
            total[...] = jnp.dot(held[...], lag_block(g, 0), preferred_element_type=jnp.float32)
            for d in range(1, n_blocks):
                part = jnp.dot(held[: size - d * rows, :], lag_block(g, d), preferred_element_type=jnp.float32)
                total[d * rows :, :] += part
        else:
            total[...] = jnp.zeros_like(total)

            @pl.loop(0, n_blocks)
            def _(d):
                shifted = held[pl.ds(pl.multiple_of(size - d * rows, rows), size), :]
                total[...] += jnp.dot(shifted, lag_block(g, d), preferred_element_type=jnp.float32)

        for i in range(n_blocks):
            direct = gain[chans, :] * held[lead + i * rows : lead + i * rows + span, :].astype(jnp.float32)
            both = (total[i * rows : i * rows + span, :] + direct).astype(jnp.bfloat16)
            for h in range(pieces):
                at = i * pieces + h
                out[at % n_fft, at // n_fft, chans, :] = both[:, h * piece : (h + 1) * piece]


def convolve(span, mixed, lags, gain, n_fft):
    n_src, n_chan, cols = mixed.shape
    n_blocks = n_src * cols // LAG
    rows = max(span, 16)
    size = n_blocks * rows
    held = size if n_blocks <= 16 else 2 * size
    vmem = pl.BlockSpec(memory_space=pltpu.VMEM)
    return pl.pallas_call(
        functools.partial(convolve_kernel, span, rows),
        out_shape=jax.ShapeDtypeStruct((n_fft, n_src, n_chan, cols // n_fft), jnp.bfloat16),
        in_specs=[vmem, vmem, vmem],
        out_specs=vmem,
        scratch_shapes=[pltpu.VMEM((held, LAG), jnp.bfloat16), pltpu.VMEM((size, LAG), jnp.float32)],
        compiler_params=pltpu.CompilerParams(vmem_limit_bytes=40 * MIB),
        cost_estimate=pl.CostEstimate(
            flops=n_chan * (n_src * cols) ** 2, bytes_accessed=2 * lags.size + 4 * mixed.size, transcendentals=0
        ),
    )(mixed, lags, gain)


def finish_kernel(place, query, conv, w0, w1, w2, w3, out, gated):
    n_fft, block, n_tok = query.shape
    for j in range(n_fft):
        product = query[j].astype(jnp.float32) * conv[j].astype(jnp.float32)
        gated[j] = product.T.astype(jnp.bfloat16)
    mine = place[0]
    width = out.shape[1]
    step = min(512, width)
    for col in range(0, width, step):
        acc = None
        for mask, w in enumerate((w0, w1, w2, w3)):
            part = jnp.dot(gated[mine ^ mask], w[:, col : col + step], preferred_element_type=jnp.float32)
            acc = part if acc is None else acc + part
        out[:, col : col + step] = acc.astype(jnp.bfloat16)


def finish(place, query, conv, weights):
    n_fft, block, n_tok = query.shape
    width = weights[0].shape[1]
    vmem = pl.BlockSpec(memory_space=pltpu.VMEM)
    return pl.pallas_call(
        finish_kernel,
        out_shape=jax.ShapeDtypeStruct((n_tok, width), jnp.bfloat16),
        in_specs=[pl.BlockSpec(memory_space=pltpu.SMEM)] + [vmem] * 6,
        out_specs=vmem,
        scratch_shapes=[pltpu.VMEM((n_fft, n_tok, block), jnp.bfloat16)],
        compiler_params=pltpu.CompilerParams(vmem_limit_bytes=24 * MIB),
        cost_estimate=pl.CostEstimate(
            flops=2 * n_fft * block * n_tok * width, bytes_accessed=2 * n_fft * block * width, transcendentals=0
        ),
    )(place, query, conv, *weights)


def body(tokens, w_in, short_taps, long_filter, skip_gain, w_out):
    n_ctx = lax.axis_size("ctx")
    n_fft = lax.axis_size("fft")
    tok_len, width = tokens.shape
    block = w_in.shape[2]
    n_groups = long_filter.shape[1]
    group_size = width // n_groups
    n_taps = short_taps.shape[0]
    ctx_index = lax.axis_index("ctx")
    fft_index = lax.axis_index("fft")
    stretch = block // n_ctx
    span = min(stretch, group_size)
    spans = stretch // span

    rim = passed_along(tokens[tok_len - RIM :], "ctx", 1)
    local_groups = block // group_size
    taps = lax.dynamic_slice_in_dim(
        short_taps.reshape(n_taps, 3, n_groups), fft_index * local_groups, local_groups, 2
    ).transpose(1, 0, 2)
    weights = w_in.transpose(1, 0, 2)
    mixed = project((1, 2), group_size, 1, rim, tokens, taps, weights)
    mixed = lax.all_to_all(mixed.reshape(n_ctx, stretch, tok_len), "ctx", 0, 0, tiled=True)

    local = lax.dynamic_slice_in_dim(long_filter, fft_index * local_groups, local_groups, 1).T
    local = jnp.repeat(local.astype(jnp.bfloat16), group_size // span, axis=0)
    filt = lax.all_to_all(local.reshape(n_ctx, spans, tok_len), "ctx", 0, 0, tiled=True)
    lags = lag_table(filt)

    query = project((0,), group_size, n_fft, rim, tokens, taps, weights)
    query = lax.all_to_all(query, "fft", 0, 0, tiled=True)

    gain = lax.dynamic_slice_in_dim(skip_gain, fft_index * block + ctx_index * stretch, stretch, 0)
    conv = convolve(span, mixed, lags, gain[:, None], n_fft)
    conv = lax.all_to_all(
        conv.reshape(n_fft * n_ctx, stretch, tok_len // n_fft), ("fft", "ctx"), 0, 0, tiled=True
    ).reshape(n_fft, block, tok_len // n_fft)

    beside = swapped(w_out, 1)
    across = swapped(w_out, 2)
    corner = swapped(across, 1)
    return finish(fft_index[None], query, conv, (w_out, beside, across, corner))


def solution(mesh):
    return jax.shard_map(
        body,
        mesh=mesh,
        in_specs=(P("ctx", None), P(None, None, "fft"), P(), P("ctx", None), P(), P("fft", None)),
        out_specs=P(("ctx", "fft"), None),
        check_vma=False,
    )
```

```python
import functools

import jax
import jax.numpy as jnp
from jax import lax
from jax.experimental import pallas as pl
from jax.experimental.pallas import tpu as pltpu
from jax.sharding import PartitionSpec as P

MIB = 1 << 20
LANES = 128
RIM = 16
LAG = 256


def fft_index():
    return lax.axis_index("chip") * lax.axis_size("core") + lax.axis_index("core")


def passed_along(block, axis, distance):
    devices = range(lax.axis_size(axis))
    route = [(i - distance, i) for i in devices if i - distance in devices]
    return lax.ppermute(block, axis, route)


def swapped(block, axis):
    return lax.ppermute(block, axis, [(i, i ^ 1) for i in range(lax.axis_size(axis))])


def spread_taps(taps, group0, group_size):
    n_taps, n_groups = taps.shape
    rows = jnp.concatenate([taps, jnp.zeros((8 - n_taps, n_groups), jnp.float32)], axis=0)
    index = group0 + lax.broadcasted_iota(jnp.int32, (8, LANES), 1) // group_size
    return jnp.take_along_axis(rows, index, axis=1, mode="promise_in_bounds")


def filtered(coef, rows_of, n_taps):
    feat = None
    for j in range(n_taps):
        term = coef[j : j + 1, :] * rows_of(j)
        feat = term if feat is None else feat + term
    return feat.astype(jnp.bfloat16).astype(jnp.float32)


def mix_kernel(group_size, sizes, tokens, taps, weights, filt, out, ext, wbuf, proj, lag, turned_lag, sems):
    stretch, chan_rows = sizes
    n_tok = tokens.shape[0]
    n_ctx = out.shape[0]
    _, n_blocks, _, width = wbuf.shape
    n_taps, n_groups = taps.shape[0], taps.shape[1] // 3
    block = n_blocks * width
    group0 = fft_index() * (block // group_size)
    main = pltpu.make_async_copy(tokens, ext, sems.at[0])
    main.start()
    loads = {}
    for blk in range(n_blocks):
        for k in range(2):
            loads[blk, k] = pltpu.make_async_copy(
                weights.at[k + 1, :, pl.ds(blk * width, width)], wbuf.at[k, blk], sems.at[2 + blk * 2 + k]
            )
            loads[blk, k].start()
    lag_load = pltpu.make_async_copy(filt, lag, sems.at[1])
    lag_load.start()
    tiles = block // LANES
    for k in range(2):
        for tile in range(tiles):
            proj[k, tile, 0:RIM, :] = jnp.zeros((RIM, LANES), jnp.float32)
    main.wait()
    chunk = min(128, n_tok)
    for blk in range(n_blocks):
        for k in range(2):
            loads[blk, k].wait()
            full = jnp.dot(ext[...], wbuf[k, blk], preferred_element_type=jnp.float32)
            full = full.astype(jnp.bfloat16).astype(jnp.float32)
            for t in range(width // LANES):
                proj[k, blk * (width // LANES) + t, RIM:, :] = full[:, t * LANES : (t + 1) * LANES]
        for t in range(width // LANES):
            tile = blk * (width // LANES) + t
            coefs = [
                spread_taps(taps[:, s * n_groups : (s + 1) * n_groups], group0 + tile * (LANES // group_size), group_size)
                for s in (1, 2)
            ]
            for row in range(0, n_tok, chunk):
                key, value = [
                    filtered(coefs[k], lambda j: proj[k, tile, RIM + row - j : RIM + row - j + chunk, :], n_taps)
                    for k in range(2)
                ]
                flipped = (key * value).T.astype(jnp.bfloat16)
                for c in range(0, LANES, stretch):
                    out[(tile * LANES + c) // stretch, 0:stretch, row : row + chunk] = flipped[c : c + stretch, :]
    lag_load.wait()
    for at in range(0, n_tok, LANES):
        turned_lag[:, at : at + LANES] = lag[at : at + LANES, :].T
    for dest in range(n_ctx):
        tile = dest * stretch // LANES
        group8 = dest * stretch // group_size // 8 * 8
        lags = turned_lag[pl.ds(pl.multiple_of(group0 + group8, 8), 8), :]
        ends = []
        for k in range(2):
            ends += [proj[k, tile, RIM : RIM + 8, :], proj[k, tile, RIM + n_tok - 8 :, :]]
        if n_tok > 4 * LANES:
            ends.append(jnp.zeros((8, n_tok - 4 * LANES), jnp.float32))
        extra = jnp.concatenate([lags, jnp.concatenate(ends, axis=1)], axis=0)
        out[dest, chan_rows:, :] = extra.astype(jnp.bfloat16)


def mix(group_size, tokens, taps, weights, filt, n_ctx):
    n_tok, depth = tokens.shape
    block = weights.shape[2]
    width = min(256, block)
    stretch = block // n_ctx
    chan_rows = -(-stretch // 16) * 16
    hbm = pl.BlockSpec(memory_space=pltpu.HBM)
    vmem = pl.BlockSpec(memory_space=pltpu.VMEM)
    return pl.pallas_call(
        functools.partial(mix_kernel, group_size, (stretch, chan_rows)),
        out_shape=jax.ShapeDtypeStruct((n_ctx, chan_rows + 16, n_tok), jnp.bfloat16),
        in_specs=[hbm, vmem, hbm, hbm],
        out_specs=vmem,
        scratch_shapes=[
            pltpu.VMEM((n_tok, depth), jnp.bfloat16),
            pltpu.VMEM((2, block // width, depth, width), jnp.bfloat16),
            pltpu.VMEM((2, block // LANES, RIM + n_tok, LANES), jnp.float32),
            pltpu.VMEM(filt.shape, jnp.float32),
            pltpu.VMEM(filt.shape[::-1], jnp.float32),
            pltpu.SemaphoreType.DMA((2 + 2 * (block // width),)),
        ],
        compiler_params=pltpu.CompilerParams(vmem_limit_bytes=56 * MIB),
        cost_estimate=pl.CostEstimate(
            flops=4 * n_tok * depth * block, bytes_accessed=2 * (n_tok * depth + 2 * depth * block), transcendentals=0
        ),
        name="mix",
    )(tokens, taps, weights, filt)


def query_kernel(group_size, rim, tokens, taps, weights, mine, other, pieces, ext, wbuf, proj, sems):
    n_tok = tokens.shape[0]
    n_blocks, _, width = wbuf.shape
    n_taps, n_groups = taps.shape[0], taps.shape[1] // 3
    piece = pieces.shape[2]
    group0 = fft_index() * (n_blocks * width // group_size)
    first = pltpu.make_async_copy(rim, ext.at[pl.ds(0, RIM)], sems.at[0])
    main = pltpu.make_async_copy(tokens, ext.at[pl.ds(RIM, n_tok)], sems.at[1])
    first.start()
    main.start()
    loads = []
    for blk in range(n_blocks):
        loads.append(
            pltpu.make_async_copy(weights.at[0, :, pl.ds(blk * width, width)], wbuf.at[blk], sems.at[2 + blk])
        )
        loads[blk].start()
    first.wait()
    main.wait()
    for blk in range(n_blocks):
        loads[blk].wait()
        full = jnp.dot(ext[...], wbuf[blk], preferred_element_type=jnp.float32)
        full = full.astype(jnp.bfloat16).astype(jnp.float32)
        for t in range(width // LANES):
            tile = blk * (width // LANES) + t
            proj[tile] = full[:, t * LANES : (t + 1) * LANES]
            coef = spread_taps(taps[:, :n_groups], group0 + tile * (LANES // group_size), group_size)
            for row in range(0, n_tok, LANES):
                feat = filtered(coef, lambda j: proj[tile, RIM + row - j : RIM + row - j + LANES, :], n_taps)
                at = row % piece
                pieces[row // piece, tile * LANES : (tile + 1) * LANES, at : at + LANES] = feat.T.astype(jnp.bfloat16)
    chip = lax.axis_index("chip")
    mine[...] = pieces[chip]
    other[...] = pieces[chip ^ 1]


def make_query(group_size, rim, tokens, taps, weights, n_chips):
    n_tok, depth = tokens.shape
    block = weights.shape[2]
    width = min(256, block)
    hbm = pl.BlockSpec(memory_space=pltpu.HBM)
    vmem = pl.BlockSpec(memory_space=pltpu.VMEM)
    return pl.pallas_call(
        functools.partial(query_kernel, group_size),
        out_shape=[jax.ShapeDtypeStruct((block, n_tok // n_chips), jnp.bfloat16)] * 2,
        in_specs=[hbm, hbm, vmem, hbm],
        out_specs=[vmem, vmem],
        scratch_shapes=[
            pltpu.VMEM((n_chips, block, n_tok // n_chips), jnp.bfloat16),
            pltpu.VMEM((RIM + n_tok, depth), jnp.bfloat16),
            pltpu.VMEM((block // width, depth, width), jnp.bfloat16),
            pltpu.VMEM((block // LANES, RIM + n_tok, LANES), jnp.float32),
            pltpu.SemaphoreType.DMA((2 + block // width,)),
        ],
        compiler_params=pltpu.CompilerParams(vmem_limit_bytes=56 * MIB),
        cost_estimate=pl.CostEstimate(
            flops=2 * n_tok * depth * block, bytes_accessed=2 * (n_tok * depth + depth * block), transcendentals=0
        ),
        name="query",
    )(rim, tokens, taps, weights)


def convolve_kernel(group_size, sizes, payload, taps, gain, out, lags, fixed, lagrow, held, total):
    stretch, chan_rows, span, rows = sizes
    n_src, _, cols = payload.shape
    n_chips, n_ctx, _, piece = out.shape
    n_taps, n_groups = taps.shape[0], taps.shape[1] // 3
    n_blocks = n_src * cols // LAG
    per_src = cols // LAG
    pieces = LAG // piece
    size = n_blocks * rows
    length = n_src * cols
    static = n_blocks <= 16
    lead = 0 if static else size
    local = lax.axis_index("ctx") * stretch
    block = stretch * n_ctx

    group0 = (fft_index() * block + local // LANES * LANES) // group_size
    coefs = [
        spread_taps(taps[:, s * n_groups : (s + 1) * n_groups], group0, group_size) for s in (1, 2)
    ]
    first = []
    for s in range(n_src):
        made = None
        for k in range(2):
            head = payload[s, chan_rows + 8 : chan_rows + 16, 2 * k * LANES : (2 * k + 1) * LANES]
            if s == 0:
                tail = jnp.zeros((8, LANES), jnp.float32)
            else:
                tail = payload[s - 1, chan_rows + 8 : chan_rows + 16, (2 * k + 1) * LANES : (2 * k + 2) * LANES]
                tail = tail.astype(jnp.float32)
            both = jnp.concatenate([tail, head.astype(jnp.float32)], axis=0)
            feat = filtered(coefs[k], lambda j: both[8 - j : 16 - j, :], n_taps)
            made = feat if made is None else made * feat
        first.append(made)
    for s in range(0, n_src, 16):
        some = first[s : s + 16]
        if len(some) < 16:
            some = some + [jnp.zeros(((16 - len(some)) * 8, LANES), jnp.float32)]
        fixed[:, s * 8 : s * 8 + LANES] = jnp.concatenate(some, axis=0).T
    chan0 = local % LANES
    lane = lax.broadcasted_iota(jnp.int32, (span, LANES), 1)

    for s in range(n_src):
        lagrow[:, s * cols : (s + 1) * cols] = payload[s, chan_rows : chan_rows + 8, :].astype(jnp.float32)
    group_in = local // group_size % 8
    zeros = jnp.zeros((1, LANES), jnp.float32)

    def lag_block(d):
        if static:
            at = d * LAG
            return jnp.concatenate([lags[:, at + LANES : at + LANES + LAG], lags[:, at : at + LAG]], axis=0)
        at = pl.multiple_of(d * LAG, LAG)
        near = lags[:, pl.ds(pl.multiple_of(at + LANES, LANES), LAG)]
        return jnp.concatenate([near, lags[:, pl.ds(at, LAG)]], axis=0)

    for g in range(stretch // span):
        row = jnp.concatenate([zeros, lagrow[pl.ds(group_in + g, 1), :], zeros], axis=1)
        wide = jnp.broadcast_to(row, (LANES, length + 2 * LANES))
        turned = pltpu.roll(wide, 0, 1, stride=1, stride_axis=0)
        lags[...] = turned[:, : length + LANES].astype(jnp.bfloat16)
        chans = slice(g * span, (g + 1) * span)
        if rows != span or lead:
            held[...] = jnp.zeros_like(held)
        for i in range(n_blocks):
            s = i // per_src
            part = payload[s, chans, (i % per_src) * LAG : (i % per_src + 1) * LAG]
            at = lead + i * rows
            held[at : at + span, :] = part
            if i % per_src == 0:
                patch = fixed[pl.ds(pl.multiple_of(chan0 + g * span, 8), span), s // 16 * LANES : (s // 16 + 1) * LANES]
                if s % 16:
                    patch = pltpu.roll(patch, LANES - s % 16 * 8, 1)
                patched = jnp.where(lane < 8, patch, part[:, :LANES].astype(jnp.float32))
                held[at : at + span, :LANES] = patched.astype(jnp.bfloat16)
        if static:
            total[...] = jnp.dot(held[...], lag_block(0), preferred_element_type=jnp.float32)
            for d in range(1, n_blocks):
                part = jnp.dot(held[: size - d * rows, :], lag_block(d), preferred_element_type=jnp.float32)
                total[d * rows :, :] += part
        else:
            total[...] = jnp.zeros_like(total)

            @pl.loop(0, n_blocks)
            def _(d):
                shifted = held[pl.ds(pl.multiple_of(size - d * rows, rows), size), :]
                total[...] += jnp.dot(shifted, lag_block(d), preferred_element_type=jnp.float32)

        for i in range(n_blocks):
            at = lead + i * rows
            direct = gain[chans, :] * held[at : at + span, :].astype(jnp.float32)
            both = (total[i * rows : i * rows + span, :] + direct).astype(jnp.bfloat16)
            for h in range(pieces):
                at = i * pieces + h
                out[at % n_chips, at // n_chips, chans, :] = both[:, h * piece : (h + 1) * piece]


def convolve(group_size, span, stretch, payload, taps, gain, n_chips):
    n_src, all_rows, cols = payload.shape
    n_blocks = n_src * cols // LAG
    rows = max(span, 16)
    size = n_blocks * rows
    length = n_src * cols
    held = size if n_blocks <= 16 else 2 * size
    vmem = pl.BlockSpec(memory_space=pltpu.VMEM)
    return pl.pallas_call(
        functools.partial(convolve_kernel, group_size, (stretch, all_rows - 16, span, rows)),
        out_shape=jax.ShapeDtypeStruct((n_chips, n_src, stretch, cols // n_chips), jnp.bfloat16),
        in_specs=[vmem, vmem, vmem],
        out_specs=vmem,
        scratch_shapes=[
            pltpu.VMEM((LANES, length + LANES), jnp.bfloat16),
            pltpu.VMEM((LANES, -(-n_src // 16) * LANES), jnp.float32),
            pltpu.VMEM((8, length), jnp.float32),
            pltpu.VMEM((held, LAG), jnp.bfloat16),
            pltpu.VMEM((size, LAG), jnp.float32),
        ],
        compiler_params=pltpu.CompilerParams(vmem_limit_bytes=48 * MIB),
        cost_estimate=pl.CostEstimate(
            flops=stretch * length**2, bytes_accessed=4 * payload.size, transcendentals=0
        ),
        name="convolve",
    )(payload, taps, gain)


def output_kernel(other_core, q_near, q_far, conv, w_near, w_far, out, gated):
    n_tok = out.shape[0]

    @pl.when(pl.program_id(0) == 0)
    def _():
        chip = lax.axis_index("chip")
        core = lax.axis_index("core") ^ other_core
        for k, query in enumerate((q_near, q_far)):
            for c in range(0, query.shape[0], LANES):
                for t in range(0, n_tok, LANES):
                    at = pl.ds(pl.multiple_of(core * n_tok + t, LANES), LANES)
                    rows = pl.ds(c, LANES)
                    product = query[rows, at].astype(jnp.float32) * conv[chip ^ k, rows, at].astype(jnp.float32)
                    gated[k, t : t + LANES, c : c + LANES] = product.T.astype(jnp.bfloat16)

    acc = jnp.dot(gated[0], w_near[...], preferred_element_type=jnp.float32)
    acc += jnp.dot(gated[1], w_far[...], preferred_element_type=jnp.float32)
    out[...] = acc.astype(out.dtype)


def output_part(other_core, dtype, query, conv, weights):
    _, block, n_tok = conv.shape
    n_tok //= 2
    width = weights[0].shape[1]
    step = min(512, width)
    vmem = pl.BlockSpec(memory_space=pltpu.VMEM)
    columns = pl.BlockSpec((block, step), lambda n: (0, n))
    return pl.pallas_call(
        functools.partial(output_kernel, other_core),
        grid=(width // step,),
        out_shape=jax.ShapeDtypeStruct((n_tok, width), dtype),
        in_specs=[vmem] * 3 + [columns] * 2,
        out_specs=pl.BlockSpec((n_tok, step), lambda n: (0, n)),
        scratch_shapes=[pltpu.VMEM((2, n_tok, block), jnp.bfloat16)],
        compiler_params=pltpu.CompilerParams(vmem_limit_bytes=24 * MIB),
        cost_estimate=pl.CostEstimate(
            flops=4 * block * n_tok * width, bytes_accessed=4 * block * width, transcendentals=0
        ),
        name="output_part",
    )(*query, conv, *weights)


def body(tokens, w_in, short_taps, long_filter, skip_gain, w_out):
    n_ctx, n_chips, n_cores = (lax.axis_size(axis) for axis in ("ctx", "chip", "core"))
    tok_len, width = tokens.shape
    block = w_in.shape[2]
    group_size = width // long_filter.shape[1]
    stretch = block // n_ctx
    span = min(stretch, group_size)
    piece = tok_len // n_chips

    weights = w_in.transpose(1, 0, 2)
    across = swapped(w_out, "chip")
    sent = mix(group_size, tokens, short_taps, weights, long_filter, n_ctx)
    payload = lax.all_to_all(sent, "ctx", 0, 0, tiled=True)

    ends, _ = lax.optimization_barrier((tokens[tok_len - RIM :], sent))
    rim = passed_along(ends, "ctx", 1)
    near, far = make_query(group_size, rim, tokens, short_taps, weights, n_chips)
    near, far, conv_taps = lax.optimization_barrier((near, far, short_taps))

    gain = lax.dynamic_slice_in_dim(skip_gain, fft_index() * block + lax.axis_index("ctx") * stretch, stretch, 0)
    conv = convolve(group_size, span, stretch, payload, conv_taps, gain[:, None], n_chips)
    far, _ = lax.optimization_barrier((far, conv))
    query = (near, swapped(far, "chip"))
    conv = lax.all_to_all(conv.reshape(n_chips * n_ctx, stretch, piece), ("chip", "ctx"), 0, 0, tiled=True)
    conv = conv.reshape(n_chips, block, piece)

    beside = swapped(output_part(1, jnp.bfloat16, query, conv, (w_out, across)), "core")
    total = output_part(0, jnp.float32, query, conv, (w_out, across))
    return (total + beside.astype(jnp.float32)).astype(jnp.bfloat16)


def solution(mesh):
    n_ctx, n_fft = (mesh.shape[axis] for axis in ("ctx", "fft"))
    split = jax.sharding.Mesh(mesh.devices.reshape(n_ctx, n_fft // 2, 2), ("ctx", "chip", "core"))
    fft = ("chip", "core")
    return jax.shard_map(
        body,
        mesh=split,
        in_specs=(P("ctx", None), P(None, None, fft), P(), P("ctx", None), P(), P(fft, None)),
        out_specs=P(("ctx",) + fft, None),
        check_vma=False,
    )
```

```python
import functools

import jax
import jax.numpy as jnp
from jax import lax
from jax.experimental import pallas as pl
from jax.experimental.pallas import tpu as pltpu
from jax.sharding import PartitionSpec as P

MIB = 1 << 20
LANES = 128
RIM = 16
LAG = 256
STAGE_FLOPS = 10**11


def fft_index():
    return lax.axis_index("chip") * lax.axis_size("core") + lax.axis_index("core")


def passed_along(block, axis, distance):
    devices = range(lax.axis_size(axis))
    route = [(i - distance, i) for i in devices if i - distance in devices]
    return lax.ppermute(block, axis, route)


def swapped(block, axis):
    return lax.ppermute(block, axis, [(i, i ^ 1) for i in range(lax.axis_size(axis))])


def spread_taps(taps, group0, group_size):
    n_taps, n_groups = taps.shape
    rows = jnp.concatenate([taps, jnp.zeros((8 - n_taps, n_groups), jnp.float32)], axis=0)
    index = group0 + lax.broadcasted_iota(jnp.int32, (8, LANES), 1) // group_size
    return jnp.take_along_axis(rows, index, axis=1, mode="promise_in_bounds")


def filtered(coef, rows_of, n_taps):
    feat = None
    for j in range(n_taps):
        term = coef[j : j + 1, :] * rows_of(j)
        feat = term if feat is None else feat + term
    return feat.astype(jnp.bfloat16).astype(jnp.float32)


def mix_kernel(group_size, tokens, taps, weights, filt, out, ext, wbuf, proj, lag, turned_lag, sems):
    n_tok = tokens.shape[0]
    n_ctx = out.shape[0]
    stretch = out.shape[1] - 8
    _, n_blocks, _, width = wbuf.shape
    n_taps, n_groups = taps.shape[0], taps.shape[1] // 3
    block = n_blocks * width
    group0 = fft_index() * (block // group_size)
    main = pltpu.make_async_copy(tokens, ext, sems.at[0])
    lag_load = pltpu.make_async_copy(filt, lag, sems.at[1])
    loads = [
        pltpu.make_async_copy(weights.at[k + 1, :, pl.ds(blk * width, width)], wbuf.at[k, blk], sems.at[2 + blk * 2 + k])
        for blk in range(n_blocks)
        for k in range(2)
    ]
    lag_load.start()
    main.start()
    for load in loads:
        load.start()
    tiles = block // LANES
    for k in range(2):
        for tile in range(tiles):
            proj[k, tile, 0:RIM, :] = jnp.zeros((RIM, LANES), jnp.float32)
    coefs = [
        [
            spread_taps(taps[:, s * n_groups : (s + 1) * n_groups], group0 + tile * (LANES // group_size), group_size)
            for tile in range(tiles)
        ]
        for s in (1, 2)
    ]
    lag_load.wait()
    for at in range(0, n_tok, LANES):
        turned_lag[:, at : at + LANES] = lag[at : at + LANES, :].T
    per_lag = n_tok // (2 * LANES)
    spans = max(1, stretch // group_size)
    for dest in range(n_ctx):
        rows = []
        for g in range(spans):
            row = turned_lag[pl.ds(group0 + dest * stretch // group_size + g, 1), :]
            rows += [row[:, h * 2 * LANES : (h + 1) * 2 * LANES] for h in range(per_lag)]
        if len(rows) < 8:
            rows.append(jnp.zeros((8 - len(rows), 2 * LANES), jnp.float32))
        out[dest, stretch:, 2 * LANES :] = jnp.concatenate(rows, axis=0).astype(jnp.bfloat16)
    chunk = min(128, n_tok)
    per_block = width // LANES

    def multiply(blk):
        for k in range(2):
            full = jnp.dot(ext[...], wbuf[k, blk], preferred_element_type=jnp.float32)
            full = full.astype(jnp.bfloat16).astype(jnp.float32)
            for t in range(per_block):
                proj[k, blk * per_block + t, RIM:, :] = full[:, t * LANES : (t + 1) * LANES]

    def finish(blk):
        for tile in range(blk * per_block, (blk + 1) * per_block):
            for row in range(0, n_tok, chunk):
                key, value = [
                    filtered(coefs[k][tile], lambda j: proj[k, tile, RIM + row - j : RIM + row - j + chunk, :], n_taps)
                    for k in range(2)
                ]
                flipped = (key * value).T.astype(jnp.bfloat16)
                for c in range(0, LANES, stretch):
                    out[(tile * LANES + c) // stretch, 0:stretch, row : row + chunk] = flipped[c : c + stretch, :]

    main.wait()
    for blk in range(n_blocks):
        for load in loads[2 * blk : 2 * blk + 2]:
            load.wait()
        multiply(blk)
        if blk:
            finish(blk - 1)
    finish(n_blocks - 1)
    low = lax.broadcasted_iota(jnp.int32, (8, LANES), 1) < LANES // 2
    for dest in range(n_ctx):
        tile, lane = divmod(dest * stretch, LANES)
        for k in range(2):
            head = proj[k, tile, RIM : RIM + 8, :]
            tail = proj[k, tile, RIM + n_tok - 8 :, :]
            if lane:
                head = pltpu.roll(head, LANES - lane, 1)
            if lane != LANES // 2:
                tail = pltpu.roll(tail, (LANES // 2 - lane) % LANES, 1)
            out[dest, stretch:, k * LANES : (k + 1) * LANES] = jnp.where(low, head, tail).astype(jnp.bfloat16)


def mix(group_size, tokens, taps, weights, filt, n_ctx):
    n_tok, depth = tokens.shape
    block = weights.shape[2]
    width = min(256, block)
    stretch = block // n_ctx
    hbm = pl.BlockSpec(memory_space=pltpu.HBM)
    vmem = pl.BlockSpec(memory_space=pltpu.VMEM)
    return pl.pallas_call(
        functools.partial(mix_kernel, group_size),
        out_shape=jax.ShapeDtypeStruct((n_ctx, stretch + 8, n_tok), jnp.bfloat16),
        in_specs=[hbm, vmem, hbm, hbm],
        out_specs=vmem,
        scratch_shapes=[
            pltpu.VMEM((n_tok, depth), jnp.bfloat16),
            pltpu.VMEM((2, block // width, depth, width), jnp.bfloat16),
            pltpu.VMEM((2, block // LANES, RIM + n_tok, LANES), jnp.float32),
            pltpu.VMEM(filt.shape, jnp.float32),
            pltpu.VMEM(filt.shape[::-1], jnp.float32),
            pltpu.SemaphoreType.DMA((2 + 2 * (block // width),)),
        ],
        compiler_params=pltpu.CompilerParams(vmem_limit_bytes=56 * MIB),
        cost_estimate=pl.CostEstimate(
            flops=4 * n_tok * depth * block, bytes_accessed=2 * (n_tok * depth + 2 * depth * block), transcendentals=0
        ),
        name="mix",
    )(tokens, taps, weights, filt)


def query_kernel(group_size, rim, tokens, taps, weights, mine, other, pieces, ext, wbuf, proj, sems):
    n_tok = tokens.shape[0]
    n_blocks, _, width = wbuf.shape
    n_taps, n_groups = taps.shape[0], taps.shape[1] // 3
    piece = pieces.shape[2]
    group0 = fft_index() * (n_blocks * width // group_size)
    first = pltpu.make_async_copy(rim, ext.at[pl.ds(0, RIM)], sems.at[0])
    main = pltpu.make_async_copy(tokens, ext.at[pl.ds(RIM, n_tok)], sems.at[1])
    first.start()
    main.start()
    loads = []
    for blk in range(n_blocks):
        loads.append(
            pltpu.make_async_copy(weights.at[0, :, pl.ds(blk * width, width)], wbuf.at[blk], sems.at[2 + blk])
        )
        loads[blk].start()
    first.wait()
    main.wait()
    for blk in range(n_blocks):
        loads[blk].wait()
        full = jnp.dot(ext[...], wbuf[blk], preferred_element_type=jnp.float32)
        full = full.astype(jnp.bfloat16).astype(jnp.float32)
        for t in range(width // LANES):
            tile = blk * (width // LANES) + t
            proj[tile] = full[:, t * LANES : (t + 1) * LANES]
            coef = spread_taps(taps[:, :n_groups], group0 + tile * (LANES // group_size), group_size)
            for row in range(0, n_tok, LANES):
                feat = filtered(coef, lambda j: proj[tile, RIM + row - j : RIM + row - j + LANES, :], n_taps)
                at = row % piece
                pieces[row // piece, tile * LANES : (tile + 1) * LANES, at : at + LANES] = feat.T.astype(jnp.bfloat16)
    chip = lax.axis_index("chip")
    mine[...] = pieces[chip]
    other[...] = pieces[chip ^ 1]


def make_query(group_size, rim, tokens, taps, weights, n_chips):
    n_tok, depth = tokens.shape
    block = weights.shape[2]
    width = min(256, block)
    hbm = pl.BlockSpec(memory_space=pltpu.HBM)
    vmem = pl.BlockSpec(memory_space=pltpu.VMEM)
    return pl.pallas_call(
        functools.partial(query_kernel, group_size),
        out_shape=[jax.ShapeDtypeStruct((block, n_tok // n_chips), jnp.bfloat16)] * 2,
        in_specs=[hbm, hbm, vmem, hbm],
        out_specs=[vmem, vmem],
        scratch_shapes=[
            pltpu.VMEM((n_chips, block, n_tok // n_chips), jnp.bfloat16),
            pltpu.VMEM((RIM + n_tok, depth), jnp.bfloat16),
            pltpu.VMEM((block // width, depth, width), jnp.bfloat16),
            pltpu.VMEM((block // LANES, RIM + n_tok, LANES), jnp.float32),
            pltpu.SemaphoreType.DMA((2 + block // width,)),
        ],
        compiler_params=pltpu.CompilerParams(vmem_limit_bytes=56 * MIB),
        cost_estimate=pl.CostEstimate(
            flops=2 * n_tok * depth * block, bytes_accessed=2 * (n_tok * depth + depth * block), transcendentals=0
        ),
        name="query",
    )(rim, tokens, taps, weights)


def convolve_kernel(group_size, sizes, payload, taps, gain, out, lags, fixed, lagrow, held, total):
    stretch, span, rows = sizes
    n_src, _, cols = payload.shape
    n_chips, n_ctx, _, piece = out.shape
    n_taps, n_groups = taps.shape[0], taps.shape[1] // 3
    n_blocks = n_src * cols // LAG
    per_src = cols // LAG
    pieces = LAG // piece
    size = n_blocks * rows
    length = n_src * cols
    static = n_blocks <= 16
    lead = 0 if static else size

    group0 = (fft_index() * stretch * n_ctx + lax.axis_index("ctx") * stretch) // group_size
    coefs = [
        spread_taps(taps[:, s * n_groups : (s + 1) * n_groups], group0, group_size) for s in (1, 2)
    ]
    ends = [[payload[s, stretch:, k * LANES : (k + 1) * LANES].astype(jnp.float32) for k in range(2)] for s in range(n_src)]
    first = []
    for s in range(n_src):
        made = None
        for k in range(2):
            before = pltpu.roll(ends[s - 1][k], LANES // 2, 1) if s else jnp.zeros((8, LANES), jnp.float32)
            both = jnp.concatenate([before, ends[s][k]], axis=0)
            feat = filtered(coefs[k], lambda j: both[8 - j : 16 - j, :], n_taps)
            made = feat if made is None else made * feat
        first.append(made)
    for s in range(0, n_src, 16):
        some = first[s : s + 16]
        if len(some) < 16:
            some = some + [jnp.zeros(((16 - len(some)) * 8, LANES), jnp.float32)]
        fixed[:, s * 8 : s * 8 + LANES] = jnp.concatenate(some, axis=0).T
    lane = lax.broadcasted_iota(jnp.int32, (span, LANES), 1)

    per_lag = cols // (2 * LANES)
    for s in range(n_src):
        piece_rows = payload[s, stretch:, 2 * LANES :].astype(jnp.float32)
        for g in range(stretch // span):
            for h in range(per_lag):
                at = s * cols + h * 2 * LANES
                lagrow[g : g + 1, at : at + 2 * LANES] = piece_rows[g * per_lag + h : g * per_lag + h + 1, :]
    zeros = jnp.zeros((1, LANES), jnp.float32)

    def lag_block(d):
        if static:
            at = d * LAG
            return jnp.concatenate([lags[:, at + LANES : at + LANES + LAG], lags[:, at : at + LAG]], axis=0)
        at = pl.multiple_of(d * LAG, LAG)
        near = lags[:, pl.ds(pl.multiple_of(at + LANES, LANES), LAG)]
        return jnp.concatenate([near, lags[:, pl.ds(at, LAG)]], axis=0)

    for g in range(stretch // span):
        row = jnp.concatenate([zeros, lagrow[g : g + 1, :], zeros], axis=1)
        wide = jnp.broadcast_to(row, (LANES, length + 2 * LANES))
        turned = pltpu.roll(wide, 0, 1, stride=1, stride_axis=0)
        lags[...] = turned[:, : length + LANES].astype(jnp.bfloat16)
        chans = slice(g * span, (g + 1) * span)
        if rows != span or lead:
            held[...] = jnp.zeros_like(held)
        for i in range(n_blocks):
            s = i // per_src
            part = payload[s, chans, (i % per_src) * LAG : (i % per_src + 1) * LAG]
            at = lead + i * rows
            held[at : at + span, :] = part
            if i % per_src == 0:
                patch = fixed[chans, s // 16 * LANES : (s // 16 + 1) * LANES]
                if s % 16:
                    patch = pltpu.roll(patch, LANES - s % 16 * 8, 1)
                patched = jnp.where(lane < 8, patch, part[:, :LANES].astype(jnp.float32))
                held[at : at + span, :LANES] = patched.astype(jnp.bfloat16)
        if static:
            total[...] = jnp.dot(held[...], lag_block(0), preferred_element_type=jnp.float32)
            for d in range(1, n_blocks):
                part = jnp.dot(held[: size - d * rows, :], lag_block(d), preferred_element_type=jnp.float32)
                total[d * rows :, :] += part
        else:
            total[...] = jnp.zeros_like(total)

            @pl.loop(0, n_blocks)
            def _(d):
                shifted = held[pl.ds(pl.multiple_of(size - d * rows, rows), size), :]
                total[...] += jnp.dot(shifted, lag_block(d), preferred_element_type=jnp.float32)

        for i in range(n_blocks):
            at = lead + i * rows
            direct = gain[chans, :] * held[at : at + span, :].astype(jnp.float32)
            both = (total[i * rows : i * rows + span, :] + direct).astype(jnp.bfloat16)
            for h in range(pieces):
                at = i * pieces + h
                out[at % n_chips, at // n_chips, chans, :] = both[:, h * piece : (h + 1) * piece]


def convolve(group_size, span, stretch, payload, taps, gain, n_chips):
    n_src, _, cols = payload.shape
    n_blocks = n_src * cols // LAG
    rows = max(span, 16)
    size = n_blocks * rows
    length = n_src * cols
    held = size if n_blocks <= 16 else 2 * size
    vmem = pl.BlockSpec(memory_space=pltpu.VMEM)
    return pl.pallas_call(
        functools.partial(convolve_kernel, group_size, (stretch, span, rows)),
        out_shape=jax.ShapeDtypeStruct((n_chips, n_src, stretch, cols // n_chips), jnp.bfloat16),
        in_specs=[vmem, vmem, vmem],
        out_specs=vmem,
        scratch_shapes=[
            pltpu.VMEM((LANES, length + LANES), jnp.bfloat16),
            pltpu.VMEM((LANES, -(-n_src // 16) * LANES), jnp.float32),
            pltpu.VMEM((8, length), jnp.float32),
            pltpu.VMEM((held, LAG), jnp.bfloat16),
            pltpu.VMEM((size, LAG), jnp.float32),
        ],
        compiler_params=pltpu.CompilerParams(vmem_limit_bytes=48 * MIB),
        cost_estimate=pl.CostEstimate(
            flops=stretch * length**2, bytes_accessed=4 * payload.size, transcendentals=0
        ),
        name="convolve",
    )(payload, taps, gain)


def stage_kernel(w_near, w_far, out, sems):
    copies = [pltpu.make_async_copy(w, out.at[k], sems.at[k]) for k, w in enumerate((w_near, w_far))]
    for copy in copies:
        copy.start()
    for copy in copies:
        copy.wait()


def stage(w_near, w_far):
    hbm = pl.BlockSpec(memory_space=pltpu.HBM)
    return pl.pallas_call(
        stage_kernel,
        out_shape=pltpu.VMEM((2,) + w_near.shape, w_near.dtype),
        in_specs=[hbm, hbm],
        out_specs=pl.BlockSpec(memory_space=pltpu.VMEM),
        scratch_shapes=[pltpu.SemaphoreType.DMA((2,))],
        compiler_params=pltpu.CompilerParams(vmem_limit_bytes=16 * MIB),
        cost_estimate=pl.CostEstimate(flops=STAGE_FLOPS, bytes_accessed=8 * w_near.size, transcendentals=0),
        name="stage",
    )(w_near, w_far)


def output_kernel(other_core, q_near, q_far, conv, weights, out):
    n_tok = out.shape[0]
    chip = lax.axis_index("chip")
    core = lax.axis_index("core") ^ other_core
    at = pl.ds(pl.multiple_of(core * n_tok, LANES), n_tok)
    gated = []
    for k, query in enumerate((q_near, q_far)):
        product = query[:, at].astype(jnp.float32) * conv[chip ^ k, :, at].astype(jnp.float32)
        gated.append(product.T.astype(jnp.bfloat16))
    width = out.shape[1]
    step = min(512, width)
    for col in range(0, width, step):
        acc = jnp.dot(gated[0], weights[0, :, col : col + step], preferred_element_type=jnp.float32)
        acc += jnp.dot(gated[1], weights[1, :, col : col + step], preferred_element_type=jnp.float32)
        out[:, col : col + step] = acc.astype(out.dtype)


def output_part(other_core, dtype, query, conv, weights):
    _, block, n_tok = conv.shape
    n_tok //= 2
    width = weights.shape[2]
    vmem = pl.BlockSpec(memory_space=pltpu.VMEM)
    return pl.pallas_call(
        functools.partial(output_kernel, other_core),
        out_shape=jax.ShapeDtypeStruct((n_tok, width), dtype),
        in_specs=[vmem] * 4,
        out_specs=vmem,
        compiler_params=pltpu.CompilerParams(vmem_limit_bytes=24 * MIB),
        cost_estimate=pl.CostEstimate(
            flops=4 * block * n_tok * width, bytes_accessed=4 * block * width, transcendentals=0
        ),
        name="output_part",
    )(*query, conv, weights)


def body(tokens, w_in, short_taps, long_filter, skip_gain, w_out):
    n_ctx, n_chips, n_cores = (lax.axis_size(axis) for axis in ("ctx", "chip", "core"))
    tok_len, width = tokens.shape
    block = w_in.shape[2]
    group_size = width // long_filter.shape[1]
    stretch = block // n_ctx
    span = min(stretch, group_size)
    piece = tok_len // n_chips

    weights = w_in.transpose(1, 0, 2)
    across = swapped(w_out, "chip")
    sent = mix(group_size, tokens, short_taps, weights, long_filter, n_ctx)
    payload = lax.all_to_all(sent, "ctx", 0, 0, tiled=True)

    ends, _ = lax.optimization_barrier((tokens[tok_len - RIM :], sent))
    rim = passed_along(ends, "ctx", 1)
    rim, conv_taps = lax.optimization_barrier((rim, short_taps))

    gain = lax.dynamic_slice_in_dim(skip_gain, fft_index() * block + lax.axis_index("ctx") * stretch, stretch, 0)
    conv = convolve(group_size, span, stretch, payload, conv_taps, gain[:, None], n_chips)

    rim, query_taps, _ = lax.optimization_barrier((rim, short_taps, conv))
    near, far = make_query(group_size, rim, tokens, query_taps, weights, n_chips)
    query = (near, swapped(far, "chip"))
    conv = lax.all_to_all(conv.reshape(n_chips * n_ctx, stretch, piece), ("chip", "ctx"), 0, 0, tiled=True)
    conv = conv.reshape(n_chips, block, piece)

    out_weights = stage(w_out, across)
    beside = swapped(output_part(1, jnp.bfloat16, query, conv, out_weights), "core")
    total = output_part(0, jnp.float32, query, conv, out_weights)
    return (total + beside.astype(jnp.float32)).astype(jnp.bfloat16)


def solution(mesh):
    n_ctx, n_fft = (mesh.shape[axis] for axis in ("ctx", "fft"))
    split = jax.sharding.Mesh(mesh.devices.reshape(n_ctx, n_fft // 2, 2), ("ctx", "chip", "core"))
    fft = ("chip", "core")
    return jax.shard_map(
        body,
        mesh=split,
        in_specs=(P("ctx", None), P(None, None, fft), P(), P("ctx", None), P(), P(fft, None)),
        out_specs=P(("ctx",) + fft, None),
        check_vma=False,
    )
```

```python
import functools

import jax
import jax.numpy as jnp
from jax import lax
from jax.experimental import pallas as pl
from jax.experimental.pallas import tpu as pltpu
from jax.sharding import PartitionSpec as P

MIB = 1 << 20
LANES = 128
RIM = 16
LAG = 256
ARRIVED_FLOPS = 10**11
ARRIVED_VMEM = 2 * MIB
OUTPUT_VMEM = 32 * MIB
CONVOLVE_FLOPS = 10**10


def fft_index():
    return lax.axis_index("chip") * lax.axis_size("core") + lax.axis_index("core")


def passed_along(block, axis, distance):
    devices = range(lax.axis_size(axis))
    route = [(i - distance, i) for i in devices if i - distance in devices]
    return lax.ppermute(block, axis, route)


def swapped(block, axis):
    return lax.ppermute(block, axis, [(i, i ^ 1) for i in range(lax.axis_size(axis))])


def spread_taps(taps, group0, group_size):
    n_taps, n_groups = taps.shape
    rows = jnp.concatenate([taps, jnp.zeros((8 - n_taps, n_groups), jnp.float32)], axis=0)
    index = group0 + lax.broadcasted_iota(jnp.int32, (8, LANES), 1) // group_size
    return jnp.take_along_axis(rows, index, axis=1, mode="promise_in_bounds")


def filtered(coef, rows_of, n_taps):
    feat = None
    for j in range(n_taps):
        term = coef[j : j + 1, :] * rows_of(j)
        feat = term if feat is None else feat + term
    return feat.astype(jnp.bfloat16).astype(jnp.float32)


def mix_kernel(group_size, tokens, taps, weights, filt, w_out, out, direct, ext, wbuf, proj, lag, turned_lag, cut, sems):
    n_tok = tokens.shape[0]
    n_ctx = out.shape[0]
    stretch = out.shape[1] - 8
    _, n_blocks, _, width = wbuf.shape
    n_taps, n_groups = taps.shape[0], taps.shape[1] // 3
    block = n_blocks * width
    group0 = fft_index() * (block // group_size)
    main = pltpu.make_async_copy(tokens, ext, sems.at[0])
    lag_load = pltpu.make_async_copy(filt, lag, sems.at[1])
    loads = [
        pltpu.make_async_copy(weights.at[k + 1, :, pl.ds(blk * width, width)], wbuf.at[k, blk], sems.at[2 + blk * 2 + k])
        for blk in range(n_blocks)
        for k in range(2)
    ]
    lag_load.start()
    main.start()
    for load in loads:
        load.start()
    tiles = block // LANES
    for k in range(2):
        for tile in range(tiles):
            proj[k, tile, 0:RIM, :] = jnp.zeros((RIM, LANES), jnp.float32)
    coefs = [
        [
            spread_taps(taps[:, s * n_groups : (s + 1) * n_groups], group0 + tile * (LANES // group_size), group_size)
            for tile in range(tiles)
        ]
        for s in (1, 2)
    ]
    lag_load.wait()
    for at in range(0, n_tok, LANES):
        turned_lag[:, at : at + LANES] = lag[at : at + LANES, :].T
    per_lag = n_tok // (2 * LANES)
    spans = max(1, stretch // group_size)
    for dest in range(n_ctx):
        rows = []
        for g in range(spans):
            row = turned_lag[pl.ds(group0 + dest * stretch // group_size + g, 1), :]
            rows += [row[:, h * 2 * LANES : (h + 1) * 2 * LANES] for h in range(per_lag)]
        if len(rows) < 8:
            rows.append(jnp.zeros((8 - len(rows), 2 * LANES), jnp.float32))
        out[dest, stretch:, 2 * LANES :] = jnp.concatenate(rows, axis=0).astype(jnp.bfloat16)
    chunk = min(128, n_tok)
    per_block = width // LANES

    def multiply(blk):
        for k in range(2):
            full = jnp.dot(ext[...], wbuf[k, blk], preferred_element_type=jnp.float32)
            full = full.astype(jnp.bfloat16).astype(jnp.float32)
            for t in range(per_block):
                proj[k, blk * per_block + t, RIM:, :] = full[:, t * LANES : (t + 1) * LANES]

    def finish(blk):
        for tile in range(blk * per_block, (blk + 1) * per_block):
            for row in range(0, n_tok, chunk):
                key, value = [
                    filtered(coefs[k][tile], lambda j: proj[k, tile, RIM + row - j : RIM + row - j + chunk, :], n_taps)
                    for k in range(2)
                ]
                flipped = (key * value).T.astype(jnp.bfloat16)
                for c in range(0, LANES, stretch):
                    out[(tile * LANES + c) // stretch, 0:stretch, row : row + chunk] = flipped[c : c + stretch, :]

    fetch = pltpu.make_async_copy(w_out.at[pl.ds(w_out.shape[0] - cut.shape[0], cut.shape[0])], cut, sems.at[2 + 2 * n_blocks])
    store = pltpu.make_async_copy(cut, direct, sems.at[3 + 2 * n_blocks])
    main.wait()
    for blk in range(n_blocks):
        for load in loads[2 * blk : 2 * blk + 2]:
            load.wait()
        if blk == n_blocks - 1:
            fetch.start()
        multiply(blk)
        if blk:
            finish(blk - 1)
    fetch.wait()
    store.start()
    finish(n_blocks - 1)
    low = lax.broadcasted_iota(jnp.int32, (8, LANES), 1) < LANES // 2
    for dest in range(n_ctx):
        tile, lane = divmod(dest * stretch, LANES)
        for k in range(2):
            head = proj[k, tile, RIM : RIM + 8, :]
            tail = proj[k, tile, RIM + n_tok - 8 :, :]
            if lane:
                head = pltpu.roll(head, LANES - lane, 1)
            if lane != LANES // 2:
                tail = pltpu.roll(tail, (LANES // 2 - lane) % LANES, 1)
            out[dest, stretch:, k * LANES : (k + 1) * LANES] = jnp.where(low, head, tail).astype(jnp.bfloat16)
    store.wait()


def mix(group_size, tokens, taps, weights, filt, w_out, rest, n_ctx):
    n_tok, depth = tokens.shape
    block = weights.shape[2]
    width = min(256, block)
    stretch = block // n_ctx
    direct = (rest, w_out.shape[1])
    hbm = pl.BlockSpec(memory_space=pltpu.HBM)
    vmem = pl.BlockSpec(memory_space=pltpu.VMEM)
    return pl.pallas_call(
        functools.partial(mix_kernel, group_size),
        out_shape=[jax.ShapeDtypeStruct(shape, jnp.bfloat16) for shape in ((n_ctx, stretch + 8, n_tok), direct)],
        in_specs=[hbm, vmem, hbm, hbm, hbm],
        out_specs=[vmem, hbm],
        scratch_shapes=[
            pltpu.VMEM((n_tok, depth), jnp.bfloat16),
            pltpu.VMEM((2, block // width, depth, width), jnp.bfloat16),
            pltpu.VMEM((2, block // LANES, RIM + n_tok, LANES), jnp.float32),
            pltpu.VMEM(filt.shape, jnp.float32),
            pltpu.VMEM(filt.shape[::-1], jnp.float32),
            pltpu.VMEM(direct, jnp.bfloat16),
            pltpu.SemaphoreType.DMA((4 + 2 * (block // width),)),
        ],
        compiler_params=pltpu.CompilerParams(vmem_limit_bytes=56 * MIB),
        cost_estimate=pl.CostEstimate(
            flops=4 * n_tok * depth * block, bytes_accessed=2 * (n_tok * depth + 2 * depth * block), transcendentals=0
        ),
        name="mix",
    )(tokens, taps, weights, filt, w_out)


def query_kernel(group_size, tokens, taps, weights, after, mine, other, ends, pieces, ext, wbuf, proj, sems):
    n_tok = tokens.shape[0]
    block = wbuf.shape[1]
    n_taps, n_groups = taps.shape[0], taps.shape[1] // 3
    piece = pieces.shape[2]
    group0 = fft_index() * (block // group_size)
    main = pltpu.make_async_copy(tokens, ext, sems.at[0])
    load = pltpu.make_async_copy(weights.at[0], wbuf, sems.at[1])
    main.start()
    load.start()
    tiles = block // LANES
    for tile in range(tiles):
        proj[tile, 0:RIM, :] = jnp.zeros((RIM, LANES), jnp.float32)
    main.wait()
    load.wait()
    full = jnp.dot(ext[...], wbuf[...], preferred_element_type=jnp.float32)
    full = full.astype(jnp.bfloat16).astype(jnp.float32)
    for tile in range(tiles):
        proj[tile, RIM:, :] = full[:, tile * LANES : (tile + 1) * LANES]
    for tile in range(tiles):
        lanes = slice(tile * LANES, (tile + 1) * LANES)
        coef = spread_taps(taps[:, :n_groups], group0 + tile * (LANES // group_size), group_size)
        both = jnp.concatenate([proj[tile, RIM + n_tok - 8 :, :], proj[tile, RIM : RIM + 8, :]], axis=0)
        ends[:, lanes] = both.astype(jnp.bfloat16)
        for row in range(0, n_tok, LANES):
            feat = filtered(coef, lambda j: proj[tile, RIM + row - j : RIM + row - j + LANES, :], n_taps)
            at = row % piece
            pieces[row // piece, lanes, at : at + LANES] = feat.T.astype(jnp.bfloat16)
    chip = lax.axis_index("chip")
    mine[...] = pieces[chip]
    other[...] = pieces[chip ^ 1]


def make_query(group_size, tokens, taps, weights, after, n_chips):
    n_tok, depth = tokens.shape
    block = weights.shape[2]
    hbm = pl.BlockSpec(memory_space=pltpu.HBM)
    vmem = pl.BlockSpec(memory_space=pltpu.VMEM)
    piece = (block, n_tok // n_chips)
    return pl.pallas_call(
        functools.partial(query_kernel, group_size),
        out_shape=[jax.ShapeDtypeStruct(shape, jnp.bfloat16) for shape in (piece, piece, (16, block))],
        in_specs=[hbm, vmem, hbm, hbm],
        out_specs=[vmem] * 3,
        scratch_shapes=[
            pltpu.VMEM((n_chips,) + piece, jnp.bfloat16),
            pltpu.VMEM((n_tok, depth), jnp.bfloat16),
            pltpu.VMEM((depth, block), jnp.bfloat16),
            pltpu.VMEM((block // LANES, RIM + n_tok, LANES), jnp.float32),
            pltpu.SemaphoreType.DMA((2,)),
        ],
        compiler_params=pltpu.CompilerParams(vmem_limit_bytes=56 * MIB),
        cost_estimate=pl.CostEstimate(
            flops=2 * n_tok * depth * block, bytes_accessed=2 * (n_tok * depth + depth * block), transcendentals=0
        ),
        name="query",
    )(tokens, taps, weights, after)


def fix_kernel(group_size, before, ends, taps, out):
    n_taps, n_groups = taps.shape[0], taps.shape[1] // 3
    block = out.shape[0]
    group0 = fft_index() * (block // group_size)
    for tile in range(block // LANES):
        lanes = slice(tile * LANES, (tile + 1) * LANES)
        coef = spread_taps(taps[:, :n_groups], group0 + tile * (LANES // group_size), group_size)
        both = jnp.concatenate(
            [before[:, lanes].astype(jnp.float32)[:8], ends[:, lanes].astype(jnp.float32)[8:]], axis=0
        )
        feat = filtered(coef, lambda j: both[8 - j : 16 - j, :], n_taps)
        feat = jnp.concatenate([feat, jnp.zeros((LANES - 8, LANES), jnp.float32)], axis=0)
        out[lanes, :] = feat.T.astype(jnp.bfloat16)


def make_fix(group_size, before, ends, taps):
    vmem = pl.BlockSpec(memory_space=pltpu.VMEM)
    return pl.pallas_call(
        functools.partial(fix_kernel, group_size),
        out_shape=jax.ShapeDtypeStruct((ends.shape[1], LANES), jnp.bfloat16),
        in_specs=[vmem] * 3,
        out_specs=vmem,
        compiler_params=pltpu.CompilerParams(vmem_limit_bytes=16 * MIB),
        cost_estimate=pl.CostEstimate(flops=10**6, bytes_accessed=10**5, transcendentals=0),
        name="fix",
    )(before, ends, taps)


def convolve_kernel(group_size, sizes, payload, taps, gain, out, lags, fixed, lagrow, held, total):
    stretch, span, rows = sizes
    n_src, _, cols = payload.shape
    n_chips, n_ctx, _, piece = out.shape
    n_taps, n_groups = taps.shape[0], taps.shape[1] // 3
    n_blocks = n_src * cols // LAG
    per_src = cols // LAG
    pieces = LAG // piece
    size = n_blocks * rows
    length = n_src * cols
    static = n_blocks <= 16
    lead = 0 if static else size

    group0 = (fft_index() * stretch * n_ctx + lax.axis_index("ctx") * stretch) // group_size
    coefs = [
        spread_taps(taps[:, s * n_groups : (s + 1) * n_groups], group0, group_size) for s in (1, 2)
    ]
    ends = [[payload[s, stretch:, k * LANES : (k + 1) * LANES].astype(jnp.float32) for k in range(2)] for s in range(n_src)]
    first = []
    for s in range(n_src):
        made = None
        for k in range(2):
            before = pltpu.roll(ends[s - 1][k], LANES // 2, 1) if s else jnp.zeros((8, LANES), jnp.float32)
            both = jnp.concatenate([before, ends[s][k]], axis=0)
            feat = filtered(coefs[k], lambda j: both[8 - j : 16 - j, :], n_taps)
            made = feat if made is None else made * feat
        first.append(made)
    for s in range(0, n_src, 16):
        some = first[s : s + 16]
        if len(some) < 16:
            some = some + [jnp.zeros(((16 - len(some)) * 8, LANES), jnp.float32)]
        fixed[:, s * 8 : s * 8 + LANES] = jnp.concatenate(some, axis=0).T
    lane = lax.broadcasted_iota(jnp.int32, (span, LANES), 1)

    per_lag = cols // (2 * LANES)
    for s in range(n_src):
        piece_rows = payload[s, stretch:, 2 * LANES :].astype(jnp.float32)
        for g in range(stretch // span):
            for h in range(per_lag):
                at = s * cols + h * 2 * LANES
                lagrow[g : g + 1, at : at + 2 * LANES] = piece_rows[g * per_lag + h : g * per_lag + h + 1, :]
    zeros = jnp.zeros((1, LANES), jnp.float32)

    def lag_block(d):
        if static:
            at = d * LAG
            return jnp.concatenate([lags[:, at + LANES : at + LANES + LAG], lags[:, at : at + LAG]], axis=0)
        at = pl.multiple_of(d * LAG, LAG)
        near = lags[:, pl.ds(pl.multiple_of(at + LANES, LANES), LAG)]
        return jnp.concatenate([near, lags[:, pl.ds(at, LAG)]], axis=0)

    for g in range(stretch // span):
        row = jnp.concatenate([zeros, lagrow[g : g + 1, :], zeros], axis=1)
        wide = jnp.broadcast_to(row, (LANES, length + 2 * LANES))
        turned = pltpu.roll(wide, 0, 1, stride=1, stride_axis=0)
        lags[...] = turned[:, : length + LANES].astype(jnp.bfloat16)
        chans = slice(g * span, (g + 1) * span)
        if rows != span or lead:
            held[...] = jnp.zeros_like(held)
        for i in range(n_blocks):
            s = i // per_src
            part = payload[s, chans, (i % per_src) * LAG : (i % per_src + 1) * LAG]
            at = lead + i * rows
            held[at : at + span, :] = part
            if i % per_src == 0:
                patch = fixed[chans, s // 16 * LANES : (s // 16 + 1) * LANES]
                if s % 16:
                    patch = pltpu.roll(patch, LANES - s % 16 * 8, 1)
                patched = jnp.where(lane < 8, patch, part[:, :LANES].astype(jnp.float32))
                held[at : at + span, :LANES] = patched.astype(jnp.bfloat16)
        if static:
            total[...] = jnp.dot(held[...], lag_block(0), preferred_element_type=jnp.float32)
            for d in range(1, n_blocks):
                part = jnp.dot(held[: size - d * rows, :], lag_block(d), preferred_element_type=jnp.float32)
                total[d * rows :, :] += part
        else:
            total[...] = jnp.zeros_like(total)

            @pl.loop(0, n_blocks)
            def _(d):
                shifted = held[pl.ds(pl.multiple_of(size - d * rows, rows), size), :]
                total[...] += jnp.dot(shifted, lag_block(d), preferred_element_type=jnp.float32)

        for i in range(n_blocks):
            at = lead + i * rows
            direct = gain[chans, :] * held[at : at + span, :].astype(jnp.float32)
            both = (total[i * rows : i * rows + span, :] + direct).astype(jnp.bfloat16)
            for h in range(pieces):
                at = i * pieces + h
                out[at % n_chips, at // n_chips, chans, :] = both[:, h * piece : (h + 1) * piece]


def convolve(group_size, span, stretch, payload, taps, gain, n_chips):
    n_src, _, cols = payload.shape
    n_blocks = n_src * cols // LAG
    rows = max(span, 16)
    size = n_blocks * rows
    length = n_src * cols
    held = size if n_blocks <= 16 else 2 * size
    vmem = pl.BlockSpec(memory_space=pltpu.VMEM)
    return pl.pallas_call(
        functools.partial(convolve_kernel, group_size, (stretch, span, rows)),
        out_shape=jax.ShapeDtypeStruct((n_chips, n_src, stretch, cols // n_chips), jnp.bfloat16),
        in_specs=[vmem, vmem, vmem],
        out_specs=vmem,
        scratch_shapes=[
            pltpu.VMEM((LANES, length + LANES), jnp.bfloat16),
            pltpu.VMEM((LANES, -(-n_src // 16) * LANES), jnp.float32),
            pltpu.VMEM((8, length), jnp.float32),
            pltpu.VMEM((held, LAG), jnp.bfloat16),
            pltpu.VMEM((size, LAG), jnp.float32),
        ],
        compiler_params=pltpu.CompilerParams(vmem_limit_bytes=48 * MIB),
        cost_estimate=pl.CostEstimate(
            flops=CONVOLVE_FLOPS, bytes_accessed=4 * payload.size, transcendentals=0
        ),
        name="convolve",
    )(payload, taps, gain)


def arrived_kernel(kept, *refs):
    refs[-1][...] = kept[...]


def arrived(kept, *blocks):
    vmem = pl.BlockSpec(memory_space=pltpu.VMEM)
    return pl.pallas_call(
        arrived_kernel,
        out_shape=jax.ShapeDtypeStruct(kept.shape, kept.dtype),
        in_specs=[vmem] + [pl.BlockSpec(memory_space=pltpu.HBM)] * len(blocks),
        out_specs=vmem,
        compiler_params=pltpu.CompilerParams(vmem_limit_bytes=ARRIVED_VMEM),
        cost_estimate=pl.CostEstimate(flops=ARRIVED_FLOPS, bytes_accessed=0, transcendentals=0),
        name="arrived",
    )(kept, *blocks)


def other_kernel(q_near, q_far, fix_near, fix_far, conv, w_near, mine, theirs, direct, other, wbuf, gated, sems):
    n_tok, width = other.shape
    block = w_near.shape[0]
    part = mine.shape[0]
    chip, core = lax.axis_index("chip"), lax.axis_index("core")
    parity = lax.axis_index("ctx") % 2
    loads = []
    for n in range(wbuf.shape[0]):
        columns = pl.ds(n * wbuf.shape[3], wbuf.shape[3])
        pairs = [(w_near, wbuf.at[n, 0])]
        for k, w in enumerate((mine, theirs)):
            pairs.append((w, wbuf.at[n, 1, pl.ds(pl.multiple_of((parity ^ k) * part, part), part)]))
        pairs.append((direct, wbuf.at[n, 1, pl.ds(2 * part, block - 2 * part)]))
        loads.append(
            [pltpu.make_async_copy(w.at[:, columns], to, sems.at[4 * n + i]) for i, (w, to) in enumerate(pairs)]
        )
    for step in loads:
        for load in step:
            load.start()
    early = lax.broadcasted_iota(jnp.int32, (block, LANES), 1) < 8

    def gate(k, half):
        query, fix = ((q_near, fix_near), (q_far, fix_far))[k]
        pieces = []
        for t in range(0, n_tok, LANES):
            at = pl.ds(pl.multiple_of((core ^ half) * n_tok + t, LANES), LANES)
            values = query[:, at].astype(jnp.float32)
            if t == 0:
                first = jnp.logical_and(early, jnp.logical_and(chip == 0, core == half))
                values = jnp.where(first, fix[...].astype(jnp.float32), values)
            product = values * conv[chip ^ k, :, at].astype(jnp.float32)
            pieces.append(product.T.astype(jnp.bfloat16))
        return pieces[0] if len(pieces) == 1 else jnp.concatenate(pieces, axis=0)

    theirs_gated = [gate(k, 1) for k in range(2)]
    for k in range(2):
        gated[k] = gate(k, 0)
    for n, step in enumerate(loads):
        for load in step:
            load.wait()
        acc = jnp.dot(theirs_gated[0], wbuf[n, 0], preferred_element_type=jnp.float32)
        acc += jnp.dot(theirs_gated[1], wbuf[n, 1], preferred_element_type=jnp.float32)
        other[:, n * wbuf.shape[3] : (n + 1) * wbuf.shape[3]] = acc.astype(other.dtype)


def other_part(query, fixes, conv, weights):
    _, block, n_tok = conv.shape
    n_tok //= 2
    width = weights[0].shape[1]
    step = width // 2
    vmem = pl.BlockSpec(memory_space=pltpu.VMEM)
    hbm = pl.BlockSpec(memory_space=pltpu.HBM)
    shapes = (n_tok, width), (width // step, 2, block, step), (2, n_tok, block)
    return pl.pallas_call(
        other_kernel,
        out_shape=[jax.ShapeDtypeStruct(shape, jnp.bfloat16) for shape in shapes],
        in_specs=[vmem] * 5 + [hbm] * 4,
        out_specs=[vmem] * 3,
        scratch_shapes=[pltpu.SemaphoreType.DMA((4 * (width // step),))],
        compiler_params=pltpu.CompilerParams(vmem_limit_bytes=OUTPUT_VMEM),
        cost_estimate=pl.CostEstimate(
            flops=4 * block * n_tok * width, bytes_accessed=4 * block * width, transcendentals=0
        ),
        name="other_part",
    )(*query, *fixes, conv, *weights)


def own_kernel(gated, weights, out):
    step = weights.shape[3]
    for n in range(weights.shape[0]):
        acc = jnp.dot(gated[0], weights[n, 0], preferred_element_type=jnp.float32)
        acc += jnp.dot(gated[1], weights[n, 1], preferred_element_type=jnp.float32)
        out[:, n * step : (n + 1) * step] = acc


def own_part(gated, weights):
    n_steps, _, block, step = weights.shape
    n_tok = gated.shape[1]
    vmem = pl.BlockSpec(memory_space=pltpu.VMEM)
    return pl.pallas_call(
        own_kernel,
        out_shape=jax.ShapeDtypeStruct((n_tok, n_steps * step), jnp.float32),
        in_specs=[vmem] * 2,
        out_specs=vmem,
        compiler_params=pltpu.CompilerParams(vmem_limit_bytes=24 * MIB),
        cost_estimate=pl.CostEstimate(
            flops=4 * block * n_tok * n_steps * step, bytes_accessed=2 * weights.size, transcendentals=0
        ),
        name="own_part",
    )(gated, weights)


def body(tokens, w_in, short_taps, long_filter, skip_gain, w_out):
    n_ctx, n_chips, n_cores = (lax.axis_size(axis) for axis in ("ctx", "chip", "core"))
    tok_len, width = tokens.shape
    block = w_in.shape[2]
    group_size = width // long_filter.shape[1]
    stretch = block // n_ctx
    span = min(stretch, group_size)
    piece = tok_len // n_chips

    weights = w_in.transpose(1, 0, 2)
    part = block // 8 * 3
    shared = lax.dynamic_slice_in_dim(w_out, lax.axis_index("ctx") % 2 * part, part, 0)
    mine = swapped(shared, "chip")
    theirs = swapped(mine, "ctx")
    sent, direct = mix(group_size, tokens, short_taps, weights, long_filter, w_out, block - 2 * part, n_ctx)
    direct = swapped(direct, "chip")
    payload = lax.all_to_all(sent, "ctx", 0, 0, tiled=True)

    near, far, ends = make_query(group_size, tokens, short_taps, weights, sent, n_chips)
    far = swapped(far, "chip")
    before = passed_along(ends, "ctx", 1)

    gain = lax.dynamic_slice_in_dim(skip_gain, fft_index() * block + lax.axis_index("ctx") * stretch, stretch, 0)
    conv = convolve(group_size, span, stretch, payload, short_taps, arrived(gain[:, None], mine, ends), n_chips)
    fix = make_fix(group_size, before, arrived(ends, far, conv), short_taps)
    conv = lax.all_to_all(conv.reshape(n_chips * n_ctx, stretch, piece), ("chip", "ctx"), 0, 0, tiled=True)
    conv = conv.reshape(n_chips, block, piece)

    fixes = (arrived(fix, theirs, direct), swapped(fix, "chip"))
    other, staged, gated = other_part((near, far), fixes, conv, (w_out, mine, theirs, direct))
    other = swapped(other, "core")
    return (own_part(gated, staged) + other.astype(jnp.float32)).astype(jnp.bfloat16)


def solution(mesh):
    n_ctx, n_fft = (mesh.shape[axis] for axis in ("ctx", "fft"))
    split = jax.sharding.Mesh(mesh.devices.reshape(n_ctx, n_fft // 2, 2), ("ctx", "chip", "core"))
    fft = ("chip", "core")
    return jax.shard_map(
        body,
        mesh=split,
        in_specs=(P("ctx", None), P(None, None, fft), P(), P("ctx", None), P(), P(fft, None)),
        out_specs=P(("ctx",) + fft, None),
        check_vma=False,
    )
```

```python
import functools

import jax
import jax.numpy as jnp
from jax import lax
from jax.experimental import pallas as pl
from jax.experimental.pallas import tpu as pltpu
from jax.sharding import PartitionSpec as P

MIB = 1 << 20
LANES = 128
RIM = 16
LAG = 256
ARRIVED_FLOPS = 10**11
ARRIVED_VMEM = 2 * MIB
OUTPUT_VMEM = 32 * MIB
CONVOLVE_FLOPS = 10**10


def fft_index():
    return lax.axis_index("chip") * lax.axis_size("core") + lax.axis_index("core")


def passed_along(block, axis, distance):
    devices = range(lax.axis_size(axis))
    route = [(i - distance, i) for i in devices if i - distance in devices]
    return lax.ppermute(block, axis, route)


def swapped(block, axis):
    return lax.ppermute(block, axis, [(i, i ^ 1) for i in range(lax.axis_size(axis))])


def spread_taps(taps, group0, group_size):
    n_taps, n_groups = taps.shape
    rows = jnp.concatenate([taps, jnp.zeros((8 - n_taps, n_groups), jnp.float32)], axis=0)
    index = group0 + lax.broadcasted_iota(jnp.int32, (8, LANES), 1) // group_size
    return jnp.take_along_axis(rows, index, axis=1, mode="promise_in_bounds")


def filtered(coef, rows_of, n_taps):
    feat = None
    for j in range(n_taps):
        term = coef[j : j + 1, :] * rows_of(j)
        feat = term if feat is None else feat + term
    return feat.astype(jnp.bfloat16).astype(jnp.float32)


def mix_kernel(group_size, tokens, taps, weights, filt, w_out, out, direct, ext, wbuf, proj, lag, turned_lag, cut, sems):
    n_tok = tokens.shape[0]
    n_ctx = out.shape[0]
    stretch = out.shape[1] - 8
    _, n_blocks, _, width = wbuf.shape
    n_taps, n_groups = taps.shape[0], taps.shape[1] // 3
    block = n_blocks * width
    group0 = fft_index() * (block // group_size)
    main = pltpu.make_async_copy(tokens, ext, sems.at[0])
    lag_load = pltpu.make_async_copy(filt, lag, sems.at[1])
    loads = [
        pltpu.make_async_copy(weights.at[k + 1, :, pl.ds(blk * width, width)], wbuf.at[k, blk], sems.at[2 + blk * 2 + k])
        for blk in range(n_blocks)
        for k in range(2)
    ]
    lag_load.start()
    main.start()
    for load in loads:
        load.start()
    tiles = block // LANES
    for k in range(2):
        for tile in range(tiles):
            proj[k, tile, 0:RIM, :] = jnp.zeros((RIM, LANES), jnp.float32)
    coefs = [
        [
            spread_taps(taps[:, s * n_groups : (s + 1) * n_groups], group0 + tile * (LANES // group_size), group_size)
            for tile in range(tiles)
        ]
        for s in (1, 2)
    ]
    lag_load.wait()
    for at in range(0, n_tok, LANES):
        turned_lag[:, at : at + LANES] = lag[at : at + LANES, :].T
    per_lag = n_tok // (2 * LANES)
    spans = max(1, stretch // group_size)
    for dest in range(n_ctx):
        rows = []
        for g in range(spans):
            row = turned_lag[pl.ds(group0 + dest * stretch // group_size + g, 1), :]
            rows += [row[:, h * 2 * LANES : (h + 1) * 2 * LANES] for h in range(per_lag)]
        if len(rows) < 8:
            rows.append(jnp.zeros((8 - len(rows), 2 * LANES), jnp.float32))
        out[dest, stretch:, 2 * LANES :] = jnp.concatenate(rows, axis=0).astype(jnp.bfloat16)
    chunk = min(128, n_tok)
    per_block = width // LANES

    def multiply(blk):
        for k in range(2):
            full = jnp.dot(ext[...], wbuf[k, blk], preferred_element_type=jnp.float32)
            full = full.astype(jnp.bfloat16).astype(jnp.float32)
            for t in range(per_block):
                proj[k, blk * per_block + t, RIM:, :] = full[:, t * LANES : (t + 1) * LANES]

    def finish(blk):
        for tile in range(blk * per_block, (blk + 1) * per_block):
            for row in range(0, n_tok, chunk):
                key, value = [
                    filtered(coefs[k][tile], lambda j: proj[k, tile, RIM + row - j : RIM + row - j + chunk, :], n_taps)
                    for k in range(2)
                ]
                flipped = (key * value).T.astype(jnp.bfloat16)
                for c in range(0, LANES, stretch):
                    out[(tile * LANES + c) // stretch, 0:stretch, row : row + chunk] = flipped[c : c + stretch, :]

    fetch = pltpu.make_async_copy(w_out.at[pl.ds(w_out.shape[0] - cut.shape[0], cut.shape[0])], cut, sems.at[2 + 2 * n_blocks])
    store = pltpu.make_async_copy(cut, direct, sems.at[3 + 2 * n_blocks])
    main.wait()
    for blk in range(n_blocks):
        for load in loads[2 * blk : 2 * blk + 2]:
            load.wait()
        if blk == n_blocks - 1:
            fetch.start()
        multiply(blk)
        if blk:
            finish(blk - 1)
    fetch.wait()
    store.start()
    finish(n_blocks - 1)
    low = lax.broadcasted_iota(jnp.int32, (8, LANES), 1) < LANES // 2
    for dest in range(n_ctx):
        tile, lane = divmod(dest * stretch, LANES)
        for k in range(2):
            head = proj[k, tile, RIM : RIM + 8, :]
            tail = proj[k, tile, RIM + n_tok - 8 :, :]
            if lane:
                head = pltpu.roll(head, LANES - lane, 1)
            if lane != LANES // 2:
                tail = pltpu.roll(tail, (LANES // 2 - lane) % LANES, 1)
            out[dest, stretch:, k * LANES : (k + 1) * LANES] = jnp.where(low, head, tail).astype(jnp.bfloat16)
    store.wait()


def mix(group_size, tokens, taps, weights, filt, w_out, rest, n_ctx):
    n_tok, depth = tokens.shape
    block = weights.shape[2]
    width = min(256, block)
    stretch = block // n_ctx
    direct = (rest, w_out.shape[1])
    hbm = pl.BlockSpec(memory_space=pltpu.HBM)
    vmem = pl.BlockSpec(memory_space=pltpu.VMEM)
    return pl.pallas_call(
        functools.partial(mix_kernel, group_size),
        out_shape=[jax.ShapeDtypeStruct(shape, jnp.bfloat16) for shape in ((n_ctx, stretch + 8, n_tok), direct)],
        in_specs=[hbm, vmem, hbm, hbm, hbm],
        out_specs=[vmem, hbm],
        scratch_shapes=[
            pltpu.VMEM((n_tok, depth), jnp.bfloat16),
            pltpu.VMEM((2, block // width, depth, width), jnp.bfloat16),
            pltpu.VMEM((2, block // LANES, RIM + n_tok, LANES), jnp.float32),
            pltpu.VMEM(filt.shape, jnp.float32),
            pltpu.VMEM(filt.shape[::-1], jnp.float32),
            pltpu.VMEM(direct, jnp.bfloat16),
            pltpu.SemaphoreType.DMA((4 + 2 * (block // width),)),
        ],
        compiler_params=pltpu.CompilerParams(vmem_limit_bytes=56 * MIB),
        cost_estimate=pl.CostEstimate(
            flops=4 * n_tok * depth * block, bytes_accessed=2 * (n_tok * depth + 2 * depth * block), transcendentals=0
        ),
        name="mix",
    )(tokens, taps, weights, filt, w_out)


def query_kernel(group_size, tokens, taps, weights, after, mine, other, ends, pieces, ext, wbuf, proj, sems):
    n_tok = tokens.shape[0]
    block = wbuf.shape[1]
    n_taps, n_groups = taps.shape[0], taps.shape[1] // 3
    piece = pieces.shape[2]
    group0 = fft_index() * (block // group_size)
    main = pltpu.make_async_copy(tokens, ext, sems.at[0])
    load = pltpu.make_async_copy(weights.at[0], wbuf, sems.at[1])
    main.start()
    load.start()
    tiles = block // LANES
    for tile in range(tiles):
        proj[tile, 0:RIM, :] = jnp.zeros((RIM, LANES), jnp.float32)
    main.wait()
    load.wait()
    full = jnp.dot(ext[...], wbuf[...], preferred_element_type=jnp.float32)
    full = full.astype(jnp.bfloat16).astype(jnp.float32)
    for tile in range(tiles):
        proj[tile, RIM:, :] = full[:, tile * LANES : (tile + 1) * LANES]
    for tile in range(tiles):
        lanes = slice(tile * LANES, (tile + 1) * LANES)
        coef = spread_taps(taps[:, :n_groups], group0 + tile * (LANES // group_size), group_size)
        both = jnp.concatenate([proj[tile, RIM + n_tok - 8 :, :], proj[tile, RIM : RIM + 8, :]], axis=0)
        ends[:, lanes] = both.astype(jnp.bfloat16)
        for row in range(0, n_tok, LANES):
            feat = filtered(coef, lambda j: proj[tile, RIM + row - j : RIM + row - j + LANES, :], n_taps)
            at = row % piece
            pieces[row // piece, lanes, at : at + LANES] = feat.T.astype(jnp.bfloat16)
    chip = lax.axis_index("chip")
    mine[...] = pieces[chip]
    other[...] = pieces[chip ^ 1]


def make_query(group_size, tokens, taps, weights, after, n_chips):
    n_tok, depth = tokens.shape
    block = weights.shape[2]
    hbm = pl.BlockSpec(memory_space=pltpu.HBM)
    vmem = pl.BlockSpec(memory_space=pltpu.VMEM)
    piece = (block, n_tok // n_chips)
    return pl.pallas_call(
        functools.partial(query_kernel, group_size),
        out_shape=[jax.ShapeDtypeStruct(shape, jnp.bfloat16) for shape in (piece, piece, (16, block))],
        in_specs=[hbm, vmem, hbm, hbm],
        out_specs=[vmem] * 3,
        scratch_shapes=[
            pltpu.VMEM((n_chips,) + piece, jnp.bfloat16),
            pltpu.VMEM((n_tok, depth), jnp.bfloat16),
            pltpu.VMEM((depth, block), jnp.bfloat16),
            pltpu.VMEM((block // LANES, RIM + n_tok, LANES), jnp.float32),
            pltpu.SemaphoreType.DMA((2,)),
        ],
        compiler_params=pltpu.CompilerParams(vmem_limit_bytes=56 * MIB),
        cost_estimate=pl.CostEstimate(
            flops=2 * n_tok * depth * block, bytes_accessed=2 * (n_tok * depth + depth * block), transcendentals=0
        ),
        name="query",
    )(tokens, taps, weights, after)


def fix_kernel(group_size, before, ends, taps, out):
    n_taps, n_groups = taps.shape[0], taps.shape[1] // 3
    block = out.shape[0]
    group0 = fft_index() * (block // group_size)
    for tile in range(block // LANES):
        lanes = slice(tile * LANES, (tile + 1) * LANES)
        coef = spread_taps(taps[:, :n_groups], group0 + tile * (LANES // group_size), group_size)
        both = jnp.concatenate(
            [before[:, lanes].astype(jnp.float32)[:8], ends[:, lanes].astype(jnp.float32)[8:]], axis=0
        )
        feat = filtered(coef, lambda j: both[8 - j : 16 - j, :], n_taps)
        feat = jnp.concatenate([feat, jnp.zeros((LANES - 8, LANES), jnp.float32)], axis=0)
        out[lanes, :] = feat.T.astype(jnp.bfloat16)


def make_fix(group_size, before, ends, taps):
    vmem = pl.BlockSpec(memory_space=pltpu.VMEM)
    return pl.pallas_call(
        functools.partial(fix_kernel, group_size),
        out_shape=jax.ShapeDtypeStruct((ends.shape[1], LANES), jnp.bfloat16),
        in_specs=[vmem] * 3,
        out_specs=vmem,
        compiler_params=pltpu.CompilerParams(vmem_limit_bytes=16 * MIB),
        cost_estimate=pl.CostEstimate(flops=10**6, bytes_accessed=10**5, transcendentals=0),
        name="fix",
    )(before, ends, taps)


def convolve_kernel(group_size, sizes, payload, taps, gain, out, lags, fixed, lagrow, held, total):
    stretch, span, rows = sizes
    n_src, _, cols = payload.shape
    n_chips, n_ctx, _, piece = out.shape
    n_taps, n_groups = taps.shape[0], taps.shape[1] // 3
    n_blocks = n_src * cols // LAG
    per_src = cols // LAG
    pieces = LAG // piece
    size = n_blocks * rows
    length = n_src * cols
    static = n_blocks <= 16
    lead = 0 if static else size

    group0 = (fft_index() * stretch * n_ctx + lax.axis_index("ctx") * stretch) // group_size
    coefs = [
        spread_taps(taps[:, s * n_groups : (s + 1) * n_groups], group0, group_size) for s in (1, 2)
    ]
    ends = [[payload[s, stretch:, k * LANES : (k + 1) * LANES].astype(jnp.float32) for k in range(2)] for s in range(n_src)]
    first = []
    for s in range(n_src):
        made = None
        for k in range(2):
            before = pltpu.roll(ends[s - 1][k], LANES // 2, 1) if s else jnp.zeros((8, LANES), jnp.float32)
            both = jnp.concatenate([before, ends[s][k]], axis=0)
            feat = filtered(coefs[k], lambda j: both[8 - j : 16 - j, :], n_taps)
            made = feat if made is None else made * feat
        first.append(made)
    for s in range(0, n_src, 16):
        some = first[s : s + 16]
        if len(some) < 16:
            some = some + [jnp.zeros(((16 - len(some)) * 8, LANES), jnp.float32)]
        fixed[:, s * 8 : s * 8 + LANES] = jnp.concatenate(some, axis=0).T
    lane = lax.broadcasted_iota(jnp.int32, (span, LANES), 1)

    per_lag = cols // (2 * LANES)
    for s in range(n_src):
        piece_rows = payload[s, stretch:, 2 * LANES :].astype(jnp.float32)
        for g in range(stretch // span):
            for h in range(per_lag):
                at = s * cols + h * 2 * LANES
                lagrow[g : g + 1, at : at + 2 * LANES] = piece_rows[g * per_lag + h : g * per_lag + h + 1, :]
    zeros = jnp.zeros((1, LANES), jnp.float32)

    def lag_block(g, d):
        if static:
            at = d * LAG
            return jnp.concatenate([lags[g, :, at + LANES : at + LANES + LAG], lags[g, :, at : at + LAG]], axis=0)
        at = pl.multiple_of(d * LAG, LAG)
        near = lags[g, :, pl.ds(pl.multiple_of(at + LANES, LANES), LAG)]
        return jnp.concatenate([near, lags[g, :, pl.ds(at, LAG)]], axis=0)

    n_spans = stretch // span

    def prepare(g):
        row = jnp.concatenate([zeros, lagrow[g : g + 1, :], zeros], axis=1)
        wide = jnp.broadcast_to(row, (LANES, length + 2 * LANES))
        turned = pltpu.roll(wide, 0, 1, stride=1, stride_axis=0)
        lags[g] = turned[:, : length + LANES].astype(jnp.bfloat16)
        chans = slice(g * span, (g + 1) * span)
        if rows != span or lead:
            held[g] = jnp.zeros(held.shape[1:], held.dtype)
        for i in range(n_blocks):
            s = i // per_src
            part = payload[s, chans, (i % per_src) * LAG : (i % per_src + 1) * LAG]
            at = lead + i * rows
            held[g, at : at + span, :] = part
            if i % per_src == 0:
                patch = fixed[chans, s // 16 * LANES : (s // 16 + 1) * LANES]
                if s % 16:
                    patch = pltpu.roll(patch, LANES - s % 16 * 8, 1)
                patched = jnp.where(lane < 8, patch, part[:, :LANES].astype(jnp.float32))
                held[g, at : at + span, :LANES] = patched.astype(jnp.bfloat16)

    def multiply(g):
        if static:
            total[g] = jnp.dot(held[g], lag_block(g, 0), preferred_element_type=jnp.float32)
            for d in range(1, n_blocks):
                part = jnp.dot(held[g, : size - d * rows, :], lag_block(g, d), preferred_element_type=jnp.float32)
                total[g, d * rows :, :] += part
        else:
            total[g] = jnp.zeros(total.shape[1:], total.dtype)

            @pl.loop(0, n_blocks)
            def _(d):
                shifted = held[g, pl.ds(pl.multiple_of(size - d * rows, rows), size), :]
                total[g] += jnp.dot(shifted, lag_block(g, d), preferred_element_type=jnp.float32)

    def store(g):
        chans = slice(g * span, (g + 1) * span)
        for i in range(n_blocks):
            at = lead + i * rows
            direct = gain[chans, :] * held[g, at : at + span, :].astype(jnp.float32)
            both = (total[g, i * rows : i * rows + span, :] + direct).astype(jnp.bfloat16)
            for h in range(pieces):
                at = i * pieces + h
                out[at % n_chips, at // n_chips, chans, :] = both[:, h * piece : (h + 1) * piece]

    prepare(0)
    for g in range(n_spans):
        if g + 1 < n_spans:
            prepare(g + 1)
        multiply(g)
        store(g)


def convolve(group_size, span, stretch, payload, taps, gain, n_chips):
    n_src, _, cols = payload.shape
    n_blocks = n_src * cols // LAG
    rows = max(span, 16)
    size = n_blocks * rows
    length = n_src * cols
    spans = stretch // span
    held = size if n_blocks <= 16 else 2 * size
    vmem = pl.BlockSpec(memory_space=pltpu.VMEM)
    return pl.pallas_call(
        functools.partial(convolve_kernel, group_size, (stretch, span, rows)),
        out_shape=jax.ShapeDtypeStruct((n_chips, n_src, stretch, cols // n_chips), jnp.bfloat16),
        in_specs=[vmem, vmem, vmem],
        out_specs=vmem,
        scratch_shapes=[
            pltpu.VMEM((spans, LANES, length + LANES), jnp.bfloat16),
            pltpu.VMEM((LANES, -(-n_src // 16) * LANES), jnp.float32),
            pltpu.VMEM((8, length), jnp.float32),
            pltpu.VMEM((spans, held, LAG), jnp.bfloat16),
            pltpu.VMEM((spans, size, LAG), jnp.float32),
        ],
        compiler_params=pltpu.CompilerParams(vmem_limit_bytes=48 * MIB),
        cost_estimate=pl.CostEstimate(
            flops=CONVOLVE_FLOPS, bytes_accessed=4 * payload.size, transcendentals=0
        ),
        name="convolve",
    )(payload, taps, gain)


def arrived_kernel(kept, *refs):
    refs[-1][...] = kept[...]


def arrived(kept, *blocks):
    vmem = pl.BlockSpec(memory_space=pltpu.VMEM)
    return pl.pallas_call(
        arrived_kernel,
        out_shape=jax.ShapeDtypeStruct(kept.shape, kept.dtype),
        in_specs=[vmem] + [pl.BlockSpec(memory_space=pltpu.HBM)] * len(blocks),
        out_specs=vmem,
        compiler_params=pltpu.CompilerParams(vmem_limit_bytes=ARRIVED_VMEM),
        cost_estimate=pl.CostEstimate(flops=ARRIVED_FLOPS, bytes_accessed=0, transcendentals=0),
        name="arrived",
    )(kept, *blocks)


def other_kernel(q_near, q_far, fix_near, fix_far, conv, w_near, mine, theirs, direct, other, wbuf, gated, sems):
    n_tok, width = other.shape
    block = w_near.shape[0]
    part = mine.shape[0]
    chip, core = lax.axis_index("chip"), lax.axis_index("core")
    parity = lax.axis_index("ctx") % 2
    loads = []
    for n in range(wbuf.shape[0]):
        columns = pl.ds(n * wbuf.shape[3], wbuf.shape[3])
        pairs = [(w_near, wbuf.at[n, 0])]
        for k, w in enumerate((mine, theirs)):
            pairs.append((w, wbuf.at[n, 1, pl.ds(pl.multiple_of((parity ^ k) * part, part), part)]))
        pairs.append((direct, wbuf.at[n, 1, pl.ds(2 * part, block - 2 * part)]))
        loads.append(
            [pltpu.make_async_copy(w.at[:, columns], to, sems.at[4 * n + i]) for i, (w, to) in enumerate(pairs)]
        )
    for step in loads:
        for load in step:
            load.start()
    early = lax.broadcasted_iota(jnp.int32, (block, LANES), 1) < 8

    def gate(k, half):
        query, fix = ((q_near, fix_near), (q_far, fix_far))[k]
        pieces = []
        for t in range(0, n_tok, LANES):
            at = pl.ds(pl.multiple_of((core ^ half) * n_tok + t, LANES), LANES)
            values = query[:, at].astype(jnp.float32)
            if t == 0:
                first = jnp.logical_and(early, jnp.logical_and(chip == 0, core == half))
                values = jnp.where(first, fix[...].astype(jnp.float32), values)
            product = values * conv[chip ^ k, :, at].astype(jnp.float32)
            pieces.append(product.T.astype(jnp.bfloat16))
        return pieces[0] if len(pieces) == 1 else jnp.concatenate(pieces, axis=0)

    theirs_gated = [gate(k, 1) for k in range(2)]
    for k in range(2):
        gated[k] = gate(k, 0)
    for n, step in enumerate(loads):
        for load in step:
            load.wait()
        acc = jnp.dot(theirs_gated[0], wbuf[n, 0], preferred_element_type=jnp.float32)
        acc += jnp.dot(theirs_gated[1], wbuf[n, 1], preferred_element_type=jnp.float32)
        other[:, n * wbuf.shape[3] : (n + 1) * wbuf.shape[3]] = acc.astype(other.dtype)


def other_part(query, fixes, conv, weights):
    _, block, n_tok = conv.shape
    n_tok //= 2
    width = weights[0].shape[1]
    step = width // 2
    vmem = pl.BlockSpec(memory_space=pltpu.VMEM)
    hbm = pl.BlockSpec(memory_space=pltpu.HBM)
    shapes = (n_tok, width), (width // step, 2, block, step), (2, n_tok, block)
    return pl.pallas_call(
        other_kernel,
        out_shape=[jax.ShapeDtypeStruct(shape, jnp.bfloat16) for shape in shapes],
        in_specs=[vmem] * 5 + [hbm] * 4,
        out_specs=[vmem] * 3,
        scratch_shapes=[pltpu.SemaphoreType.DMA((4 * (width // step),))],
        compiler_params=pltpu.CompilerParams(vmem_limit_bytes=OUTPUT_VMEM),
        cost_estimate=pl.CostEstimate(
            flops=4 * block * n_tok * width, bytes_accessed=4 * block * width, transcendentals=0
        ),
        name="other_part",
    )(*query, *fixes, conv, *weights)


def own_kernel(gated, weights, out):
    step = weights.shape[3]
    for n in range(weights.shape[0]):
        acc = jnp.dot(gated[0], weights[n, 0], preferred_element_type=jnp.float32)
        acc += jnp.dot(gated[1], weights[n, 1], preferred_element_type=jnp.float32)
        out[:, n * step : (n + 1) * step] = acc


def own_part(gated, weights):
    n_steps, _, block, step = weights.shape
    n_tok = gated.shape[1]
    vmem = pl.BlockSpec(memory_space=pltpu.VMEM)
    return pl.pallas_call(
        own_kernel,
        out_shape=jax.ShapeDtypeStruct((n_tok, n_steps * step), jnp.float32),
        in_specs=[vmem] * 2,
        out_specs=vmem,
        compiler_params=pltpu.CompilerParams(vmem_limit_bytes=24 * MIB),
        cost_estimate=pl.CostEstimate(
            flops=4 * block * n_tok * n_steps * step, bytes_accessed=2 * weights.size, transcendentals=0
        ),
        name="own_part",
    )(gated, weights)


def body(tokens, w_in, short_taps, long_filter, skip_gain, w_out):
    n_ctx, n_chips, n_cores = (lax.axis_size(axis) for axis in ("ctx", "chip", "core"))
    tok_len, width = tokens.shape
    block = w_in.shape[2]
    group_size = width // long_filter.shape[1]
    stretch = block // n_ctx
    span = min(stretch, group_size)
    piece = tok_len // n_chips

    weights = w_in.transpose(1, 0, 2)
    part = block // 8 * 3
    shared = lax.dynamic_slice_in_dim(w_out, lax.axis_index("ctx") % 2 * part, part, 0)
    mine = swapped(shared, "chip")
    theirs = swapped(mine, "ctx")
    sent, direct = mix(group_size, tokens, short_taps, weights, long_filter, w_out, block - 2 * part, n_ctx)
    direct = swapped(direct, "chip")
    payload = lax.all_to_all(sent, "ctx", 0, 0, tiled=True)

    near, far, ends = make_query(group_size, tokens, short_taps, weights, sent, n_chips)
    far = swapped(far, "chip")
    before = passed_along(ends, "ctx", 1)

    gain = lax.dynamic_slice_in_dim(skip_gain, fft_index() * block + lax.axis_index("ctx") * stretch, stretch, 0)
    conv = convolve(group_size, span, stretch, payload, short_taps, arrived(gain[:, None], mine, ends), n_chips)
    fix = make_fix(group_size, before, arrived(ends, far, conv), short_taps)
    conv = lax.all_to_all(conv.reshape(n_chips * n_ctx, stretch, piece), ("chip", "ctx"), 0, 0, tiled=True)
    conv = conv.reshape(n_chips, block, piece)

    fixes = (arrived(fix, theirs, direct), swapped(fix, "chip"))
    other, staged, gated = other_part((near, far), fixes, conv, (w_out, mine, theirs, direct))
    other = swapped(other, "core")
    return (own_part(gated, staged) + other.astype(jnp.float32)).astype(jnp.bfloat16)


def solution(mesh):
    n_ctx, n_fft = (mesh.shape[axis] for axis in ("ctx", "fft"))
    split = jax.sharding.Mesh(mesh.devices.reshape(n_ctx, n_fft // 2, 2), ("ctx", "chip", "core"))
    fft = ("chip", "core")
    return jax.shard_map(
        body,
        mesh=split,
        in_specs=(P("ctx", None), P(None, None, fft), P(), P("ctx", None), P(), P(fft, None)),
        out_specs=P(("ctx",) + fft, None),
        check_vma=False,
    )
```

```python
import functools

import jax
import jax.numpy as jnp
from jax import lax
from jax.experimental import pallas as pl
from jax.experimental.pallas import tpu as pltpu
from jax.sharding import PartitionSpec as P

MIB = 1 << 20
LANES = 128
RIM = 16
LAG = 256
ARRIVED_FLOPS = 10**11
ARRIVED_VMEM = 2 * MIB
OUTPUT_VMEM = 32 * MIB
CONVOLVE_FLOPS = 10**10


def fft_index():
    return lax.axis_index("chip") * lax.axis_size("core") + lax.axis_index("core")


def passed_along(block, axis, distance):
    devices = range(lax.axis_size(axis))
    route = [(i - distance, i) for i in devices if i - distance in devices]
    return lax.ppermute(block, axis, route)


def swapped(block, axis):
    return lax.ppermute(block, axis, [(i, i ^ 1) for i in range(lax.axis_size(axis))])


def spread_taps(taps, group0, group_size):
    n_taps, n_groups = taps.shape
    rows = jnp.concatenate([taps, jnp.zeros((8 - n_taps, n_groups), jnp.float32)], axis=0)
    index = group0 + lax.broadcasted_iota(jnp.int32, (8, LANES), 1) // group_size
    return jnp.take_along_axis(rows, index, axis=1, mode="promise_in_bounds")


def filtered(coef, rows_of, n_taps):
    feat = None
    for j in range(n_taps):
        term = coef[j : j + 1, :] * rows_of(j)
        feat = term if feat is None else feat + term
    return feat.astype(jnp.bfloat16).astype(jnp.float32)


def mix_kernel(group_size, tokens, taps, weights, filt, w_out, out, shared, direct, ext, wbuf, proj, lag, turned_lag, cut, sems):
    n_tok = tokens.shape[0]
    n_ctx = out.shape[0]
    stretch = out.shape[1] - 8
    _, n_blocks, _, width = wbuf.shape
    n_taps, n_groups = taps.shape[0], taps.shape[1] // 3
    block = n_blocks * width
    group0 = fft_index() * (block // group_size)
    main = pltpu.make_async_copy(tokens, ext, sems.at[0])
    lag_load = pltpu.make_async_copy(filt, lag, sems.at[1])
    loads = [
        pltpu.make_async_copy(weights.at[k + 1, :, pl.ds(blk * width, width)], wbuf.at[k, blk], sems.at[2 + blk * 2 + k])
        for blk in range(n_blocks)
        for k in range(2)
    ]
    lag_load.start()
    main.start()
    for load in loads:
        load.start()
    tiles = block // LANES
    for k in range(2):
        for tile in range(tiles):
            proj[k, tile, 0:RIM, :] = jnp.zeros((RIM, LANES), jnp.float32)
    coefs = [
        [
            spread_taps(taps[:, s * n_groups : (s + 1) * n_groups], group0 + tile * (LANES // group_size), group_size)
            for tile in range(tiles)
        ]
        for s in (1, 2)
    ]
    lag_load.wait()
    for at in range(0, n_tok, LANES):
        turned_lag[:, at : at + LANES] = lag[at : at + LANES, :].T
    per_lag = n_tok // (2 * LANES)
    spans = max(1, stretch // group_size)
    for dest in range(n_ctx):
        rows = []
        for g in range(spans):
            row = turned_lag[pl.ds(group0 + dest * stretch // group_size + g, 1), :]
            rows += [row[:, h * 2 * LANES : (h + 1) * 2 * LANES] for h in range(per_lag)]
        if len(rows) < 8:
            rows.append(jnp.zeros((8 - len(rows), 2 * LANES), jnp.float32))
        out[dest, stretch:, 2 * LANES :] = jnp.concatenate(rows, axis=0).astype(jnp.bfloat16)
    chunk = min(128, n_tok)
    per_block = width // LANES

    def multiply(blk):
        for k in range(2):
            full = jnp.dot(ext[...], wbuf[k, blk], preferred_element_type=jnp.float32)
            full = full.astype(jnp.bfloat16).astype(jnp.float32)
            for t in range(per_block):
                proj[k, blk * per_block + t, RIM:, :] = full[:, t * LANES : (t + 1) * LANES]

    def finish(blk):
        for tile in range(blk * per_block, (blk + 1) * per_block):
            for row in range(0, n_tok, chunk):
                key, value = [
                    filtered(coefs[k][tile], lambda j: proj[k, tile, RIM + row - j : RIM + row - j + chunk, :], n_taps)
                    for k in range(2)
                ]
                flipped = (key * value).T.astype(jnp.bfloat16)
                for c in range(0, LANES, stretch):
                    out[(tile * LANES + c) // stretch, 0:stretch, row : row + chunk] = flipped[c : c + stretch, :]

    part, rest = shared.shape[0], direct.shape[0]
    parity = lax.axis_index("ctx") % 2
    base = 2 + 2 * n_blocks
    fetches = [
        pltpu.make_async_copy(
            w_out.at[pl.ds(pl.multiple_of(parity * part, part), part)], cut.at[pl.ds(0, part)], sems.at[base]
        ),
        pltpu.make_async_copy(w_out.at[pl.ds(2 * part, rest)], cut.at[pl.ds(part, rest)], sems.at[base + 1]),
    ]
    stores = [
        pltpu.make_async_copy(cut.at[pl.ds(0, part)], shared, sems.at[base + 2]),
        pltpu.make_async_copy(cut.at[pl.ds(part, rest)], direct, sems.at[base + 3]),
    ]
    main.wait()
    for blk in range(n_blocks):
        for load in loads[2 * blk : 2 * blk + 2]:
            load.wait()
        if blk == n_blocks - 1:
            for fetch in fetches:
                fetch.start()
        multiply(blk)
        if blk:
            finish(blk - 1)
    for fetch, store in zip(fetches, stores):
        fetch.wait()
        store.start()
    finish(n_blocks - 1)
    low = lax.broadcasted_iota(jnp.int32, (8, LANES), 1) < LANES // 2
    for dest in range(n_ctx):
        tile, lane = divmod(dest * stretch, LANES)
        for k in range(2):
            head = proj[k, tile, RIM : RIM + 8, :]
            tail = proj[k, tile, RIM + n_tok - 8 :, :]
            if lane:
                head = pltpu.roll(head, LANES - lane, 1)
            if lane != LANES // 2:
                tail = pltpu.roll(tail, (LANES // 2 - lane) % LANES, 1)
            out[dest, stretch:, k * LANES : (k + 1) * LANES] = jnp.where(low, head, tail).astype(jnp.bfloat16)
    for store in stores:
        store.wait()


def mix(group_size, tokens, taps, weights, filt, w_out, part, n_ctx):
    n_tok, depth = tokens.shape
    block = weights.shape[2]
    width = min(256, block)
    stretch = block // n_ctx
    rest = block - 2 * part
    parts = [(rows, w_out.shape[1]) for rows in (part, rest)]
    hbm = pl.BlockSpec(memory_space=pltpu.HBM)
    vmem = pl.BlockSpec(memory_space=pltpu.VMEM)
    return pl.pallas_call(
        functools.partial(mix_kernel, group_size),
        out_shape=[jax.ShapeDtypeStruct(shape, jnp.bfloat16) for shape in [(n_ctx, stretch + 8, n_tok)] + parts],
        in_specs=[hbm, vmem, hbm, hbm, hbm],
        out_specs=[vmem, hbm, hbm],
        scratch_shapes=[
            pltpu.VMEM((n_tok, depth), jnp.bfloat16),
            pltpu.VMEM((2, block // width, depth, width), jnp.bfloat16),
            pltpu.VMEM((2, block // LANES, RIM + n_tok, LANES), jnp.float32),
            pltpu.VMEM(filt.shape, jnp.float32),
            pltpu.VMEM(filt.shape[::-1], jnp.float32),
            pltpu.VMEM((part + rest, w_out.shape[1]), jnp.bfloat16),
            pltpu.SemaphoreType.DMA((6 + 2 * (block // width),)),
        ],
        compiler_params=pltpu.CompilerParams(vmem_limit_bytes=56 * MIB),
        cost_estimate=pl.CostEstimate(
            flops=4 * n_tok * depth * block, bytes_accessed=2 * (n_tok * depth + 2 * depth * block), transcendentals=0
        ),
        name="mix",
    )(tokens, taps, weights, filt, w_out)


def query_kernel(group_size, tokens, taps, weights, after, mine, other, ends, pieces, ext, wbuf, proj, sems):
    n_tok = tokens.shape[0]
    block = wbuf.shape[1]
    n_taps, n_groups = taps.shape[0], taps.shape[1] // 3
    piece = pieces.shape[2]
    group0 = fft_index() * (block // group_size)
    main = pltpu.make_async_copy(tokens, ext, sems.at[0])
    load = pltpu.make_async_copy(weights.at[0], wbuf, sems.at[1])
    main.start()
    load.start()
    tiles = block // LANES
    for tile in range(tiles):
        proj[tile, 0:RIM, :] = jnp.zeros((RIM, LANES), jnp.float32)
    main.wait()
    load.wait()
    full = jnp.dot(ext[...], wbuf[...], preferred_element_type=jnp.float32)
    full = full.astype(jnp.bfloat16).astype(jnp.float32)
    for tile in range(tiles):
        proj[tile, RIM:, :] = full[:, tile * LANES : (tile + 1) * LANES]
    for tile in range(tiles):
        lanes = slice(tile * LANES, (tile + 1) * LANES)
        coef = spread_taps(taps[:, :n_groups], group0 + tile * (LANES // group_size), group_size)
        both = jnp.concatenate([proj[tile, RIM + n_tok - 8 :, :], proj[tile, RIM : RIM + 8, :]], axis=0)
        ends[:, lanes] = both.astype(jnp.bfloat16)
        for row in range(0, n_tok, LANES):
            feat = filtered(coef, lambda j: proj[tile, RIM + row - j : RIM + row - j + LANES, :], n_taps)
            at = row % piece
            pieces[row // piece, lanes, at : at + LANES] = feat.T.astype(jnp.bfloat16)
    chip = lax.axis_index("chip")
    mine[...] = pieces[chip]
    other[...] = pieces[chip ^ 1]


def make_query(group_size, tokens, taps, weights, after, n_chips):
    n_tok, depth = tokens.shape
    block = weights.shape[2]
    hbm = pl.BlockSpec(memory_space=pltpu.HBM)
    vmem = pl.BlockSpec(memory_space=pltpu.VMEM)
    piece = (block, n_tok // n_chips)
    return pl.pallas_call(
        functools.partial(query_kernel, group_size),
        out_shape=[jax.ShapeDtypeStruct(shape, jnp.bfloat16) for shape in (piece, piece, (16, block))],
        in_specs=[hbm, vmem, hbm, hbm],
        out_specs=[vmem] * 3,
        scratch_shapes=[
            pltpu.VMEM((n_chips,) + piece, jnp.bfloat16),
            pltpu.VMEM((n_tok, depth), jnp.bfloat16),
            pltpu.VMEM((depth, block), jnp.bfloat16),
            pltpu.VMEM((block // LANES, RIM + n_tok, LANES), jnp.float32),
            pltpu.SemaphoreType.DMA((2,)),
        ],
        compiler_params=pltpu.CompilerParams(vmem_limit_bytes=56 * MIB),
        cost_estimate=pl.CostEstimate(
            flops=2 * n_tok * depth * block, bytes_accessed=2 * (n_tok * depth + depth * block), transcendentals=0
        ),
        name="query",
    )(tokens, taps, weights, after)


def fix_kernel(group_size, before, ends, taps, out):
    n_taps, n_groups = taps.shape[0], taps.shape[1] // 3
    block = out.shape[1]
    group0 = fft_index() * (block // group_size)
    for tile in range(block // LANES):
        lanes = slice(tile * LANES, (tile + 1) * LANES)
        coef = spread_taps(taps[:, :n_groups], group0 + tile * (LANES // group_size), group_size)
        both = jnp.concatenate(
            [before[:, lanes].astype(jnp.float32)[:8], ends[:, lanes].astype(jnp.float32)[8:]], axis=0
        )
        feat = filtered(coef, lambda j: both[8 - j : 16 - j, :], n_taps)
        out[:, lanes] = jnp.concatenate([feat, jnp.zeros((8, LANES), jnp.float32)], axis=0).astype(jnp.bfloat16)


def make_fix(group_size, before, ends, taps):
    vmem = pl.BlockSpec(memory_space=pltpu.VMEM)
    return pl.pallas_call(
        functools.partial(fix_kernel, group_size),
        out_shape=jax.ShapeDtypeStruct(ends.shape, jnp.bfloat16),
        in_specs=[vmem] * 3,
        out_specs=vmem,
        compiler_params=pltpu.CompilerParams(vmem_limit_bytes=16 * MIB),
        cost_estimate=pl.CostEstimate(flops=10**6, bytes_accessed=10**5, transcendentals=0),
        name="fix",
    )(before, ends, taps)


def convolve_kernel(group_size, sizes, payload, taps, gain, out, lags, fixed, lagrow, held, total):
    stretch, span, rows = sizes
    n_src, _, cols = payload.shape
    n_chips, n_ctx, _, piece = out.shape
    n_taps, n_groups = taps.shape[0], taps.shape[1] // 3
    n_blocks = n_src * cols // LAG
    per_src = cols // LAG
    pieces = LAG // piece
    size = n_blocks * rows
    length = n_src * cols
    static = n_blocks <= 16
    lead = 0 if static else size

    group0 = (fft_index() * stretch * n_ctx + lax.axis_index("ctx") * stretch) // group_size
    coefs = [
        spread_taps(taps[:, s * n_groups : (s + 1) * n_groups], group0, group_size) for s in (1, 2)
    ]
    ends = [[payload[s, stretch:, k * LANES : (k + 1) * LANES].astype(jnp.float32) for k in range(2)] for s in range(n_src)]
    first = []
    for s in range(n_src):
        made = None
        for k in range(2):
            before = pltpu.roll(ends[s - 1][k], LANES // 2, 1) if s else jnp.zeros((8, LANES), jnp.float32)
            both = jnp.concatenate([before, ends[s][k]], axis=0)
            feat = filtered(coefs[k], lambda j: both[8 - j : 16 - j, :], n_taps)
            made = feat if made is None else made * feat
        first.append(made)
    for s in range(0, n_src, 16):
        some = first[s : s + 16]
        if len(some) < 16:
            some = some + [jnp.zeros(((16 - len(some)) * 8, LANES), jnp.float32)]
        fixed[:, s * 8 : s * 8 + LANES] = jnp.concatenate(some, axis=0).T
    lane = lax.broadcasted_iota(jnp.int32, (span, LANES), 1)

    per_lag = cols // (2 * LANES)
    for s in range(n_src):
        piece_rows = payload[s, stretch:, 2 * LANES :].astype(jnp.float32)
        for g in range(stretch // span):
            for h in range(per_lag):
                at = s * cols + h * 2 * LANES
                lagrow[g : g + 1, at : at + 2 * LANES] = piece_rows[g * per_lag + h : g * per_lag + h + 1, :]
    zeros = jnp.zeros((1, LANES), jnp.float32)

    def lag_block(g, d):
        if static:
            at = d * LAG
            return jnp.concatenate([lags[g, :, at + LANES : at + LANES + LAG], lags[g, :, at : at + LAG]], axis=0)
        at = pl.multiple_of(d * LAG, LAG)
        near = lags[g, :, pl.ds(pl.multiple_of(at + LANES, LANES), LAG)]
        return jnp.concatenate([near, lags[g, :, pl.ds(at, LAG)]], axis=0)

    n_spans = stretch // span

    def prepare(g):
        row = jnp.concatenate([zeros, lagrow[g : g + 1, :], zeros], axis=1)
        wide = jnp.broadcast_to(row, (LANES, length + 2 * LANES))
        turned = pltpu.roll(wide, 0, 1, stride=1, stride_axis=0)
        lags[g] = turned[:, : length + LANES].astype(jnp.bfloat16)
        chans = slice(g * span, (g + 1) * span)
        if rows != span or lead:
            held[g] = jnp.zeros(held.shape[1:], held.dtype)
        for i in range(n_blocks):
            s = i // per_src
            part = payload[s, chans, (i % per_src) * LAG : (i % per_src + 1) * LAG]
            at = lead + i * rows
            held[g, at : at + span, :] = part
            if i % per_src == 0:
                patch = fixed[chans, s // 16 * LANES : (s // 16 + 1) * LANES]
                if s % 16:
                    patch = pltpu.roll(patch, LANES - s % 16 * 8, 1)
                patched = jnp.where(lane < 8, patch, part[:, :LANES].astype(jnp.float32))
                held[g, at : at + span, :LANES] = patched.astype(jnp.bfloat16)

    def multiply(g):
        if static:
            total[g] = jnp.dot(held[g], lag_block(g, 0), preferred_element_type=jnp.float32)
            for d in range(1, n_blocks):
                part = jnp.dot(held[g, : size - d * rows, :], lag_block(g, d), preferred_element_type=jnp.float32)
                total[g, d * rows :, :] += part
        else:
            total[g] = jnp.zeros(total.shape[1:], total.dtype)

            @pl.loop(0, n_blocks)
            def _(d):
                shifted = held[g, pl.ds(pl.multiple_of(size - d * rows, rows), size), :]
                total[g] += jnp.dot(shifted, lag_block(g, d), preferred_element_type=jnp.float32)

    def store(g):
        chans = slice(g * span, (g + 1) * span)
        for i in range(n_blocks):
            at = lead + i * rows
            direct = gain[chans, :] * held[g, at : at + span, :].astype(jnp.float32)
            both = (total[g, i * rows : i * rows + span, :] + direct).astype(jnp.bfloat16)
            for h in range(pieces):
                at = i * pieces + h
                out[at % n_chips, at // n_chips, chans, :] = both[:, h * piece : (h + 1) * piece]

    prepare(0)
    for g in range(n_spans):
        if g + 1 < n_spans:
            prepare(g + 1)
        multiply(g)
        store(g)


def convolve(group_size, span, stretch, payload, taps, gain, n_chips):
    n_src, _, cols = payload.shape
    n_blocks = n_src * cols // LAG
    rows = max(span, 16)
    size = n_blocks * rows
    length = n_src * cols
    spans = stretch // span
    held = size if n_blocks <= 16 else 2 * size
    vmem = pl.BlockSpec(memory_space=pltpu.VMEM)
    return pl.pallas_call(
        functools.partial(convolve_kernel, group_size, (stretch, span, rows)),
        out_shape=jax.ShapeDtypeStruct((n_chips, n_src, stretch, cols // n_chips), jnp.bfloat16),
        in_specs=[vmem, vmem, vmem],
        out_specs=vmem,
        scratch_shapes=[
            pltpu.VMEM((spans, LANES, length + LANES), jnp.bfloat16),
            pltpu.VMEM((LANES, -(-n_src // 16) * LANES), jnp.float32),
            pltpu.VMEM((8, length), jnp.float32),
            pltpu.VMEM((spans, held, LAG), jnp.bfloat16),
            pltpu.VMEM((spans, size, LAG), jnp.float32),
        ],
        compiler_params=pltpu.CompilerParams(vmem_limit_bytes=48 * MIB),
        cost_estimate=pl.CostEstimate(
            flops=CONVOLVE_FLOPS, bytes_accessed=4 * payload.size, transcendentals=0
        ),
        name="convolve",
    )(payload, taps, gain)


def arrived_kernel(kept, *refs):
    refs[-1][...] = kept[...]


def arrived(kept, *blocks):
    vmem = pl.BlockSpec(memory_space=pltpu.VMEM)
    return pl.pallas_call(
        arrived_kernel,
        out_shape=jax.ShapeDtypeStruct(kept.shape, kept.dtype),
        in_specs=[vmem] + [pl.BlockSpec(memory_space=pltpu.HBM)] * len(blocks),
        out_specs=vmem,
        compiler_params=pltpu.CompilerParams(vmem_limit_bytes=ARRIVED_VMEM),
        cost_estimate=pl.CostEstimate(flops=ARRIVED_FLOPS, bytes_accessed=0, transcendentals=0),
        name="arrived",
    )(kept, *blocks)


def other_kernel(q_near, q_far, fix_near, fix_far, conv, w_near, mine, theirs, direct, other, wbuf, gated, sems):
    n_tok, width = other.shape
    block = w_near.shape[0]
    part = mine.shape[0]
    chip, core = lax.axis_index("chip"), lax.axis_index("core")
    parity = lax.axis_index("ctx") % 2
    loads = []
    for n in range(wbuf.shape[0]):
        columns = pl.ds(n * wbuf.shape[3], wbuf.shape[3])
        pairs = [(w_near, wbuf.at[n, 0])]
        for k, w in enumerate((mine, theirs)):
            pairs.append((w, wbuf.at[n, 1, pl.ds(pl.multiple_of((parity ^ k) * part, part), part)]))
        pairs.append((direct, wbuf.at[n, 1, pl.ds(2 * part, block - 2 * part)]))
        loads.append(
            [pltpu.make_async_copy(w.at[:, columns], to, sems.at[4 * n + i]) for i, (w, to) in enumerate(pairs)]
        )
    for step in loads:
        for load in step:
            load.start()
    early = lax.broadcasted_iota(jnp.int32, (block, LANES), 1) < 8

    def channels_first(fix):
        rows = jnp.concatenate([fix[...].astype(jnp.float32), jnp.zeros((LANES - 16, block), jnp.float32)], axis=0)
        return jnp.concatenate([rows[:, at : at + LANES].T for at in range(0, block, LANES)], axis=0)

    fixes = [channels_first(fix) for fix in (fix_near, fix_far)]

    def gate(k, half):
        query = (q_near, q_far)[k]
        pieces = []
        for t in range(0, n_tok, LANES):
            at = pl.ds(pl.multiple_of((core ^ half) * n_tok + t, LANES), LANES)
            values = query[:, at].astype(jnp.float32)
            if t == 0:
                first = jnp.logical_and(early, jnp.logical_and(chip == 0, core == half))
                values = jnp.where(first, fixes[k], values)
            product = values * conv[chip ^ k, :, at].astype(jnp.float32)
            pieces.append(product.T.astype(jnp.bfloat16))
        return pieces[0] if len(pieces) == 1 else jnp.concatenate(pieces, axis=0)

    theirs_gated = [gate(k, 1) for k in range(2)]
    for k in range(2):
        gated[k] = gate(k, 0)
    for n, step in enumerate(loads):
        for load in step:
            load.wait()
        acc = jnp.dot(theirs_gated[0], wbuf[n, 0], preferred_element_type=jnp.float32)
        acc += jnp.dot(theirs_gated[1], wbuf[n, 1], preferred_element_type=jnp.float32)
        other[:, n * wbuf.shape[3] : (n + 1) * wbuf.shape[3]] = acc.astype(other.dtype)


def other_part(query, fixes, conv, weights):
    _, block, n_tok = conv.shape
    n_tok //= 2
    width = weights[0].shape[1]
    step = width // 2
    vmem = pl.BlockSpec(memory_space=pltpu.VMEM)
    hbm = pl.BlockSpec(memory_space=pltpu.HBM)
    shapes = (n_tok, width), (width // step, 2, block, step), (2, n_tok, block)
    return pl.pallas_call(
        other_kernel,
        out_shape=[jax.ShapeDtypeStruct(shape, jnp.bfloat16) for shape in shapes],
        in_specs=[vmem] * 5 + [hbm] * 4,
        out_specs=[vmem] * 3,
        scratch_shapes=[pltpu.SemaphoreType.DMA((4 * (width // step),))],
        compiler_params=pltpu.CompilerParams(vmem_limit_bytes=OUTPUT_VMEM),
        cost_estimate=pl.CostEstimate(
            flops=4 * block * n_tok * width, bytes_accessed=4 * block * width, transcendentals=0
        ),
        name="other_part",
    )(*query, *fixes, conv, *weights)


def own_kernel(gated, weights, out):
    step = weights.shape[3]
    for n in range(weights.shape[0]):
        acc = jnp.dot(gated[0], weights[n, 0], preferred_element_type=jnp.float32)
        acc += jnp.dot(gated[1], weights[n, 1], preferred_element_type=jnp.float32)
        out[:, n * step : (n + 1) * step] = acc


def own_part(gated, weights):
    n_steps, _, block, step = weights.shape
    n_tok = gated.shape[1]
    vmem = pl.BlockSpec(memory_space=pltpu.VMEM)
    return pl.pallas_call(
        own_kernel,
        out_shape=jax.ShapeDtypeStruct((n_tok, n_steps * step), jnp.float32),
        in_specs=[vmem] * 2,
        out_specs=vmem,
        compiler_params=pltpu.CompilerParams(vmem_limit_bytes=24 * MIB),
        cost_estimate=pl.CostEstimate(
            flops=4 * block * n_tok * n_steps * step, bytes_accessed=2 * weights.size, transcendentals=0
        ),
        name="own_part",
    )(gated, weights)


def body(tokens, w_in, short_taps, long_filter, skip_gain, w_out):
    n_ctx, n_chips, n_cores = (lax.axis_size(axis) for axis in ("ctx", "chip", "core"))
    tok_len, width = tokens.shape
    block = w_in.shape[2]
    group_size = width // long_filter.shape[1]
    stretch = block // n_ctx
    span = min(stretch, group_size)
    piece = tok_len // n_chips

    weights = w_in.transpose(1, 0, 2)
    sent, shared, direct = mix(
        group_size, tokens, short_taps, weights, long_filter, w_out, block // 32 * 12, n_ctx
    )
    mine, direct = swapped(shared, "chip"), swapped(direct, "chip")
    theirs = swapped(mine, "ctx")
    payload = lax.all_to_all(sent, "ctx", 0, 0, tiled=True)

    near, far, ends = make_query(group_size, tokens, short_taps, weights, sent, n_chips)
    far = swapped(far, "chip")
    before = passed_along(ends, "ctx", 1)

    gain = lax.dynamic_slice_in_dim(skip_gain, fft_index() * block + lax.axis_index("ctx") * stretch, stretch, 0)
    conv = convolve(group_size, span, stretch, payload, short_taps, arrived(gain[:, None], mine, ends), n_chips)
    fix = make_fix(group_size, before, arrived(ends, conv), short_taps)
    conv = lax.all_to_all(conv.reshape(n_chips * n_ctx, stretch, piece), ("chip", "ctx"), 0, 0, tiled=True)
    conv = conv.reshape(n_chips, block, piece)

    fixes = (arrived(fix, theirs, direct, far), swapped(fix, "chip"))
    other, staged, gated = other_part((near, far), fixes, conv, (w_out, mine, theirs, direct))
    other = swapped(other, "core")
    return (own_part(gated, staged) + other.astype(jnp.float32)).astype(jnp.bfloat16)


def solution(mesh):
    n_ctx, n_fft = (mesh.shape[axis] for axis in ("ctx", "fft"))
    split = jax.sharding.Mesh(mesh.devices.reshape(n_ctx, n_fft // 2, 2), ("ctx", "chip", "core"))
    fft = ("chip", "core")
    return jax.shard_map(
        body,
        mesh=split,
        in_specs=(P("ctx", None), P(None, None, fft), P(), P("ctx", None), P(), P(fft, None)),
        out_specs=P(("ctx",) + fft, None),
        check_vma=False,
    )
```

```python
import functools

import jax
import jax.numpy as jnp
from jax import lax
from jax.experimental import pallas as pl
from jax.experimental.pallas import tpu as pltpu
from jax.sharding import PartitionSpec as P

MIB = 1 << 20
LANES = 128
RIM = 16
LAG = 256
ARRIVED_FLOPS = 10**11
ARRIVED_VMEM = 2 * MIB
OUTPUT_VMEM = 32 * MIB
CONVOLVE_FLOPS = 10**10


def fft_index():
    return lax.axis_index("chip") * lax.axis_size("core") + lax.axis_index("core")


def passed_along(block, axis, distance):
    devices = range(lax.axis_size(axis))
    route = [(i - distance, i) for i in devices if i - distance in devices]
    return lax.ppermute(block, axis, route)


def swapped(block, axis):
    return lax.ppermute(block, axis, [(i, i ^ 1) for i in range(lax.axis_size(axis))])


def spread_taps(taps, group0, group_size):
    n_taps, n_groups = taps.shape
    rows = jnp.concatenate([taps, jnp.zeros((8 - n_taps, n_groups), jnp.float32)], axis=0)
    index = group0 + lax.broadcasted_iota(jnp.int32, (8, LANES), 1) // group_size
    return jnp.take_along_axis(rows, index, axis=1, mode="promise_in_bounds")


def filtered(coef, rows_of, n_taps):
    feat = None
    for j in range(n_taps):
        term = coef[j : j + 1, :] * rows_of(j)
        feat = term if feat is None else feat + term
    return feat.astype(jnp.bfloat16).astype(jnp.float32)


def mix_kernel(group_size, tokens, taps, weights, filt, w_out, out, shared, ext, wbuf, proj, lag, turned_lag, cut, sems):
    n_tok = tokens.shape[0]
    n_ctx = out.shape[0]
    stretch = out.shape[1] - 8
    _, n_blocks, _, width = wbuf.shape
    n_taps, n_groups = taps.shape[0], taps.shape[1] // 3
    block = n_blocks * width
    group0 = fft_index() * (block // group_size)
    main = pltpu.make_async_copy(tokens, ext, sems.at[0])
    lag_load = pltpu.make_async_copy(filt, lag, sems.at[1])
    loads = [
        pltpu.make_async_copy(weights.at[k + 1, :, pl.ds(blk * width, width)], wbuf.at[k, blk], sems.at[2 + blk * 2 + k])
        for blk in range(n_blocks)
        for k in range(2)
    ]
    lag_load.start()
    main.start()
    for load in loads:
        load.start()
    tiles = block // LANES
    for k in range(2):
        for tile in range(tiles):
            proj[k, tile, 0:RIM, :] = jnp.zeros((RIM, LANES), jnp.float32)
    coefs = [
        [
            spread_taps(taps[:, s * n_groups : (s + 1) * n_groups], group0 + tile * (LANES // group_size), group_size)
            for tile in range(tiles)
        ]
        for s in (1, 2)
    ]
    lag_load.wait()
    for at in range(0, n_tok, LANES):
        turned_lag[:, at : at + LANES] = lag[at : at + LANES, :].T
    per_lag = n_tok // (2 * LANES)
    spans = max(1, stretch // group_size)
    for dest in range(n_ctx):
        rows = []
        for g in range(spans):
            row = turned_lag[pl.ds(group0 + dest * stretch // group_size + g, 1), :]
            rows += [row[:, h * 2 * LANES : (h + 1) * 2 * LANES] for h in range(per_lag)]
        if len(rows) < 8:
            rows.append(jnp.zeros((8 - len(rows), 2 * LANES), jnp.float32))
        out[dest, stretch:, 2 * LANES :] = jnp.concatenate(rows, axis=0).astype(jnp.bfloat16)
    chunk = min(128, n_tok)
    per_block = width // LANES

    def multiply(blk):
        for k in range(2):
            full = jnp.dot(ext[...], wbuf[k, blk], preferred_element_type=jnp.float32)
            full = full.astype(jnp.bfloat16).astype(jnp.float32)
            for t in range(per_block):
                proj[k, blk * per_block + t, RIM:, :] = full[:, t * LANES : (t + 1) * LANES]

    def finish(blk):
        for tile in range(blk * per_block, (blk + 1) * per_block):
            for row in range(0, n_tok, chunk):
                key, value = [
                    filtered(coefs[k][tile], lambda j: proj[k, tile, RIM + row - j : RIM + row - j + chunk, :], n_taps)
                    for k in range(2)
                ]
                flipped = (key * value).T.astype(jnp.bfloat16)
                for c in range(0, LANES, stretch):
                    out[(tile * LANES + c) // stretch, 0:stretch, row : row + chunk] = flipped[c : c + stretch, :]

    part = shared.shape[0]
    parity = lax.axis_index("ctx") % 2
    fetch = pltpu.make_async_copy(
        w_out.at[pl.ds(pl.multiple_of(parity * part, part), part)], cut, sems.at[2 + 2 * n_blocks]
    )
    store = pltpu.make_async_copy(cut, shared, sems.at[3 + 2 * n_blocks])
    main.wait()
    for blk in range(n_blocks):
        for load in loads[2 * blk : 2 * blk + 2]:
            load.wait()
        if blk == n_blocks - 1:
            fetch.start()
        multiply(blk)
        if blk:
            finish(blk - 1)
    fetch.wait()
    store.start()
    finish(n_blocks - 1)
    low = lax.broadcasted_iota(jnp.int32, (8, LANES), 1) < LANES // 2
    for dest in range(n_ctx):
        tile, lane = divmod(dest * stretch, LANES)
        for k in range(2):
            head = proj[k, tile, RIM : RIM + 8, :]
            tail = proj[k, tile, RIM + n_tok - 8 :, :]
            if lane:
                head = pltpu.roll(head, LANES - lane, 1)
            if lane != LANES // 2:
                tail = pltpu.roll(tail, (LANES // 2 - lane) % LANES, 1)
            out[dest, stretch:, k * LANES : (k + 1) * LANES] = jnp.where(low, head, tail).astype(jnp.bfloat16)
    store.wait()


def mix(group_size, tokens, taps, weights, filt, w_out, part, n_ctx):
    n_tok, depth = tokens.shape
    block = weights.shape[2]
    width = min(256, block)
    stretch = block // n_ctx
    shared = (part, w_out.shape[1])
    hbm = pl.BlockSpec(memory_space=pltpu.HBM)
    vmem = pl.BlockSpec(memory_space=pltpu.VMEM)
    return pl.pallas_call(
        functools.partial(mix_kernel, group_size),
        out_shape=[jax.ShapeDtypeStruct(shape, jnp.bfloat16) for shape in ((n_ctx, stretch + 8, n_tok), shared)],
        in_specs=[hbm, vmem, hbm, hbm, hbm],
        out_specs=[vmem, hbm],
        scratch_shapes=[
            pltpu.VMEM((n_tok, depth), jnp.bfloat16),
            pltpu.VMEM((2, block // width, depth, width), jnp.bfloat16),
            pltpu.VMEM((2, block // LANES, RIM + n_tok, LANES), jnp.float32),
            pltpu.VMEM(filt.shape, jnp.float32),
            pltpu.VMEM(filt.shape[::-1], jnp.float32),
            pltpu.VMEM(shared, jnp.bfloat16),
            pltpu.SemaphoreType.DMA((4 + 2 * (block // width),)),
        ],
        compiler_params=pltpu.CompilerParams(vmem_limit_bytes=56 * MIB),
        cost_estimate=pl.CostEstimate(
            flops=4 * n_tok * depth * block, bytes_accessed=2 * (n_tok * depth + 2 * depth * block), transcendentals=0
        ),
        name="mix",
    )(tokens, taps, weights, filt, w_out)


def query_kernel(group_size, tokens, taps, weights, w_out, after, mine, other, ends, direct, pieces, ext, wbuf, proj, cut, sems):
    n_tok = tokens.shape[0]
    block = wbuf.shape[1]
    n_taps, n_groups = taps.shape[0], taps.shape[1] // 3
    piece = pieces.shape[2]
    group0 = fft_index() * (block // group_size)
    main = pltpu.make_async_copy(tokens, ext, sems.at[0])
    load = pltpu.make_async_copy(weights.at[0], wbuf, sems.at[1])
    rest = direct.shape[0]
    fetch = pltpu.make_async_copy(w_out.at[pl.ds(w_out.shape[0] - rest, rest)], cut, sems.at[2])
    store = pltpu.make_async_copy(cut, direct, sems.at[3])
    main.start()
    load.start()
    fetch.start()
    tiles = block // LANES
    for tile in range(tiles):
        proj[tile, 0:RIM, :] = jnp.zeros((RIM, LANES), jnp.float32)
    main.wait()
    load.wait()
    fetch.wait()
    store.start()
    full = jnp.dot(ext[...], wbuf[...], preferred_element_type=jnp.float32)
    full = full.astype(jnp.bfloat16).astype(jnp.float32)
    for tile in range(tiles):
        proj[tile, RIM:, :] = full[:, tile * LANES : (tile + 1) * LANES]
    for tile in range(tiles):
        lanes = slice(tile * LANES, (tile + 1) * LANES)
        coef = spread_taps(taps[:, :n_groups], group0 + tile * (LANES // group_size), group_size)
        both = jnp.concatenate([proj[tile, RIM + n_tok - 8 :, :], proj[tile, RIM : RIM + 8, :]], axis=0)
        ends[:, lanes] = both.astype(jnp.bfloat16)
        for row in range(0, n_tok, LANES):
            feat = filtered(coef, lambda j: proj[tile, RIM + row - j : RIM + row - j + LANES, :], n_taps)
            at = row % piece
            pieces[row // piece, lanes, at : at + LANES] = feat.T.astype(jnp.bfloat16)
    chip = lax.axis_index("chip")
    mine[...] = pieces[chip]
    other[...] = pieces[chip ^ 1]
    store.wait()


def make_query(group_size, tokens, taps, weights, w_out, rest, after, n_chips):
    n_tok, depth = tokens.shape
    block = weights.shape[2]
    hbm = pl.BlockSpec(memory_space=pltpu.HBM)
    vmem = pl.BlockSpec(memory_space=pltpu.VMEM)
    piece = (block, n_tok // n_chips)
    direct = (rest, w_out.shape[1])
    return pl.pallas_call(
        functools.partial(query_kernel, group_size),
        out_shape=[jax.ShapeDtypeStruct(shape, jnp.bfloat16) for shape in (piece, piece, (16, block), direct)],
        in_specs=[hbm, vmem, hbm, hbm, hbm],
        out_specs=[vmem] * 3 + [hbm],
        scratch_shapes=[
            pltpu.VMEM((n_chips,) + piece, jnp.bfloat16),
            pltpu.VMEM((n_tok, depth), jnp.bfloat16),
            pltpu.VMEM((depth, block), jnp.bfloat16),
            pltpu.VMEM((block // LANES, RIM + n_tok, LANES), jnp.float32),
            pltpu.VMEM(direct, jnp.bfloat16),
            pltpu.SemaphoreType.DMA((4,)),
        ],
        compiler_params=pltpu.CompilerParams(vmem_limit_bytes=56 * MIB),
        cost_estimate=pl.CostEstimate(
            flops=2 * n_tok * depth * block, bytes_accessed=2 * (n_tok * depth + depth * block), transcendentals=0
        ),
        name="query",
    )(tokens, taps, weights, w_out, after)


def fix_kernel(group_size, before, ends, taps, out):
    n_taps, n_groups = taps.shape[0], taps.shape[1] // 3
    block = out.shape[1]
    group0 = fft_index() * (block // group_size)
    for tile in range(block // LANES):
        lanes = slice(tile * LANES, (tile + 1) * LANES)
        coef = spread_taps(taps[:, :n_groups], group0 + tile * (LANES // group_size), group_size)
        both = jnp.concatenate(
            [before[:, lanes].astype(jnp.float32)[:8], ends[:, lanes].astype(jnp.float32)[8:]], axis=0
        )
        feat = filtered(coef, lambda j: both[8 - j : 16 - j, :], n_taps)
        out[:, lanes] = jnp.concatenate([feat, jnp.zeros((8, LANES), jnp.float32)], axis=0).astype(jnp.bfloat16)


def make_fix(group_size, before, ends, taps):
    vmem = pl.BlockSpec(memory_space=pltpu.VMEM)
    return pl.pallas_call(
        functools.partial(fix_kernel, group_size),
        out_shape=jax.ShapeDtypeStruct(ends.shape, jnp.bfloat16),
        in_specs=[vmem] * 3,
        out_specs=vmem,
        compiler_params=pltpu.CompilerParams(vmem_limit_bytes=16 * MIB),
        cost_estimate=pl.CostEstimate(flops=10**6, bytes_accessed=10**5, transcendentals=0),
        name="fix",
    )(before, ends, taps)


def convolve_kernel(group_size, sizes, payload, taps, gain, out, lags, fixed, lagrow, held, total):
    stretch, span, rows = sizes
    n_src, _, cols = payload.shape
    n_chips, n_ctx, _, piece = out.shape
    n_taps, n_groups = taps.shape[0], taps.shape[1] // 3
    n_blocks = n_src * cols // LAG
    per_src = cols // LAG
    pieces = LAG // piece
    size = n_blocks * rows
    length = n_src * cols
    static = n_blocks <= 16
    lead = 0 if static else size

    group0 = (fft_index() * stretch * n_ctx + lax.axis_index("ctx") * stretch) // group_size
    coefs = [
        spread_taps(taps[:, s * n_groups : (s + 1) * n_groups], group0, group_size) for s in (1, 2)
    ]
    ends = [[payload[s, stretch:, k * LANES : (k + 1) * LANES].astype(jnp.float32) for k in range(2)] for s in range(n_src)]
    first = []
    for s in range(n_src):
        made = None
        for k in range(2):
            before = pltpu.roll(ends[s - 1][k], LANES // 2, 1) if s else jnp.zeros((8, LANES), jnp.float32)
            both = jnp.concatenate([before, ends[s][k]], axis=0)
            feat = filtered(coefs[k], lambda j: both[8 - j : 16 - j, :], n_taps)
            made = feat if made is None else made * feat
        first.append(made)
    for s in range(0, n_src, 16):
        some = first[s : s + 16]
        if len(some) < 16:
            some = some + [jnp.zeros(((16 - len(some)) * 8, LANES), jnp.float32)]
        fixed[:, s * 8 : s * 8 + LANES] = jnp.concatenate(some, axis=0).T
    lane = lax.broadcasted_iota(jnp.int32, (span, LANES), 1)

    per_lag = cols // (2 * LANES)
    for s in range(n_src):
        piece_rows = payload[s, stretch:, 2 * LANES :].astype(jnp.float32)
        for g in range(stretch // span):
            for h in range(per_lag):
                at = s * cols + h * 2 * LANES
                lagrow[g : g + 1, at : at + 2 * LANES] = piece_rows[g * per_lag + h : g * per_lag + h + 1, :]
    zeros = jnp.zeros((1, LANES), jnp.float32)

    def lag_block(g, d):
        if static:
            at = d * LAG
            return jnp.concatenate([lags[g, :, at + LANES : at + LANES + LAG], lags[g, :, at : at + LAG]], axis=0)
        at = pl.multiple_of(d * LAG, LAG)
        near = lags[g, :, pl.ds(pl.multiple_of(at + LANES, LANES), LAG)]
        return jnp.concatenate([near, lags[g, :, pl.ds(at, LAG)]], axis=0)

    n_spans = stretch // span

    def prepare(g):
        row = jnp.concatenate([zeros, lagrow[g : g + 1, :], zeros], axis=1)
        wide = jnp.broadcast_to(row, (LANES, length + 2 * LANES))
        turned = pltpu.roll(wide, 0, 1, stride=1, stride_axis=0)
        lags[g] = turned[:, : length + LANES].astype(jnp.bfloat16)
        chans = slice(g * span, (g + 1) * span)
        if rows != span or lead:
            held[g] = jnp.zeros(held.shape[1:], held.dtype)
        for i in range(n_blocks):
            s = i // per_src
            part = payload[s, chans, (i % per_src) * LAG : (i % per_src + 1) * LAG]
            at = lead + i * rows
            held[g, at : at + span, :] = part
            if i % per_src == 0:
                patch = fixed[chans, s // 16 * LANES : (s // 16 + 1) * LANES]
                if s % 16:
                    patch = pltpu.roll(patch, LANES - s % 16 * 8, 1)
                patched = jnp.where(lane < 8, patch, part[:, :LANES].astype(jnp.float32))
                held[g, at : at + span, :LANES] = patched.astype(jnp.bfloat16)

    def multiply(g):
        if static:
            total[g] = jnp.dot(held[g], lag_block(g, 0), preferred_element_type=jnp.float32)
            for d in range(1, n_blocks):
                part = jnp.dot(held[g, : size - d * rows, :], lag_block(g, d), preferred_element_type=jnp.float32)
                total[g, d * rows :, :] += part
        else:
            total[g] = jnp.zeros(total.shape[1:], total.dtype)

            @pl.loop(0, n_blocks)
            def _(d):
                shifted = held[g, pl.ds(pl.multiple_of(size - d * rows, rows), size), :]
                total[g] += jnp.dot(shifted, lag_block(g, d), preferred_element_type=jnp.float32)

    def store(g):
        chans = slice(g * span, (g + 1) * span)
        for i in range(n_blocks):
            at = lead + i * rows
            direct = gain[chans, :] * held[g, at : at + span, :].astype(jnp.float32)
            both = (total[g, i * rows : i * rows + span, :] + direct).astype(jnp.bfloat16)
            for h in range(pieces):
                at = i * pieces + h
                out[at % n_chips, at // n_chips, chans, :] = both[:, h * piece : (h + 1) * piece]

    prepare(0)
    for g in range(n_spans):
        if g + 1 < n_spans:
            prepare(g + 1)
        multiply(g)
        store(g)


def convolve(group_size, span, stretch, payload, taps, gain, n_chips):
    n_src, _, cols = payload.shape
    n_blocks = n_src * cols // LAG
    rows = max(span, 16)
    size = n_blocks * rows
    length = n_src * cols
    spans = stretch // span
    held = size if n_blocks <= 16 else 2 * size
    vmem = pl.BlockSpec(memory_space=pltpu.VMEM)
    return pl.pallas_call(
        functools.partial(convolve_kernel, group_size, (stretch, span, rows)),
        out_shape=jax.ShapeDtypeStruct((n_chips, n_src, stretch, cols // n_chips), jnp.bfloat16),
        in_specs=[vmem, vmem, vmem],
        out_specs=vmem,
        scratch_shapes=[
            pltpu.VMEM((spans, LANES, length + LANES), jnp.bfloat16),
            pltpu.VMEM((LANES, -(-n_src // 16) * LANES), jnp.float32),
            pltpu.VMEM((8, length), jnp.float32),
            pltpu.VMEM((spans, held, LAG), jnp.bfloat16),
            pltpu.VMEM((spans, size, LAG), jnp.float32),
        ],
        compiler_params=pltpu.CompilerParams(vmem_limit_bytes=48 * MIB),
        cost_estimate=pl.CostEstimate(
            flops=CONVOLVE_FLOPS, bytes_accessed=4 * payload.size, transcendentals=0
        ),
        name="convolve",
    )(payload, taps, gain)


def arrived_kernel(kept, *refs):
    refs[-1][...] = kept[...]


def arrived(kept, *blocks):
    vmem = pl.BlockSpec(memory_space=pltpu.VMEM)
    return pl.pallas_call(
        arrived_kernel,
        out_shape=jax.ShapeDtypeStruct(kept.shape, kept.dtype),
        in_specs=[vmem] + [pl.BlockSpec(memory_space=pltpu.HBM)] * len(blocks),
        out_specs=vmem,
        compiler_params=pltpu.CompilerParams(vmem_limit_bytes=ARRIVED_VMEM),
        cost_estimate=pl.CostEstimate(flops=ARRIVED_FLOPS, bytes_accessed=0, transcendentals=0),
        name="arrived",
    )(kept, *blocks)


def other_kernel(q_near, q_far, fix_near, fix_far, conv, w_near, mine, theirs, direct, other, wbuf, gated, sems):
    n_tok, width = other.shape
    block = w_near.shape[0]
    part = mine.shape[0]
    chip, core = lax.axis_index("chip"), lax.axis_index("core")
    parity = lax.axis_index("ctx") % 2
    loads = []
    for n in range(wbuf.shape[0]):
        columns = pl.ds(n * wbuf.shape[3], wbuf.shape[3])
        pairs = [(w_near, wbuf.at[n, 0])]
        for k, w in enumerate((mine, theirs)):
            pairs.append((w, wbuf.at[n, 1, pl.ds(pl.multiple_of((parity ^ k) * part, part), part)]))
        pairs.append((direct, wbuf.at[n, 1, pl.ds(2 * part, block - 2 * part)]))
        loads.append(
            [pltpu.make_async_copy(w.at[:, columns], to, sems.at[4 * n + i]) for i, (w, to) in enumerate(pairs)]
        )
    for step in loads:
        for load in step:
            load.start()
    early = lax.broadcasted_iota(jnp.int32, (block, LANES), 1) < 8

    def channels_first(fix):
        rows = jnp.concatenate([fix[...].astype(jnp.float32), jnp.zeros((LANES - 16, block), jnp.float32)], axis=0)
        return jnp.concatenate([rows[:, at : at + LANES].T for at in range(0, block, LANES)], axis=0)

    fixes = [channels_first(fix) for fix in (fix_near, fix_far)]

    def gate(k, half):
        query = (q_near, q_far)[k]
        pieces = []
        for t in range(0, n_tok, LANES):
            at = pl.ds(pl.multiple_of((core ^ half) * n_tok + t, LANES), LANES)
            values = query[:, at].astype(jnp.float32)
            if t == 0:
                first = jnp.logical_and(early, jnp.logical_and(chip == 0, core == half))
                values = jnp.where(first, fixes[k], values)
            product = values * conv[chip ^ k, :, at].astype(jnp.float32)
            pieces.append(product.T.astype(jnp.bfloat16))
        return pieces[0] if len(pieces) == 1 else jnp.concatenate(pieces, axis=0)

    theirs_gated = [gate(k, 1) for k in range(2)]
    for k in range(2):
        gated[k] = gate(k, 0)
    for n, step in enumerate(loads):
        for load in step:
            load.wait()
        acc = jnp.dot(theirs_gated[0], wbuf[n, 0], preferred_element_type=jnp.float32)
        acc += jnp.dot(theirs_gated[1], wbuf[n, 1], preferred_element_type=jnp.float32)
        other[:, n * wbuf.shape[3] : (n + 1) * wbuf.shape[3]] = acc.astype(other.dtype)


def other_part(query, fixes, conv, weights):
    _, block, n_tok = conv.shape
    n_tok //= 2
    width = weights[0].shape[1]
    step = width // 2
    vmem = pl.BlockSpec(memory_space=pltpu.VMEM)
    hbm = pl.BlockSpec(memory_space=pltpu.HBM)
    shapes = (n_tok, width), (width // step, 2, block, step), (2, n_tok, block)
    return pl.pallas_call(
        other_kernel,
        out_shape=[jax.ShapeDtypeStruct(shape, jnp.bfloat16) for shape in shapes],
        in_specs=[vmem] * 5 + [hbm] * 4,
        out_specs=[vmem] * 3,
        scratch_shapes=[pltpu.SemaphoreType.DMA((4 * (width // step),))],
        compiler_params=pltpu.CompilerParams(vmem_limit_bytes=OUTPUT_VMEM),
        cost_estimate=pl.CostEstimate(
            flops=4 * block * n_tok * width, bytes_accessed=4 * block * width, transcendentals=0
        ),
        name="other_part",
    )(*query, *fixes, conv, *weights)


def own_kernel(gated, weights, out):
    step = weights.shape[3]
    for n in range(weights.shape[0]):
        acc = jnp.dot(gated[0], weights[n, 0], preferred_element_type=jnp.float32)
        acc += jnp.dot(gated[1], weights[n, 1], preferred_element_type=jnp.float32)
        out[:, n * step : (n + 1) * step] = acc


def own_part(gated, weights):
    n_steps, _, block, step = weights.shape
    n_tok = gated.shape[1]
    vmem = pl.BlockSpec(memory_space=pltpu.VMEM)
    return pl.pallas_call(
        own_kernel,
        out_shape=jax.ShapeDtypeStruct((n_tok, n_steps * step), jnp.float32),
        in_specs=[vmem] * 2,
        out_specs=vmem,
        compiler_params=pltpu.CompilerParams(vmem_limit_bytes=24 * MIB),
        cost_estimate=pl.CostEstimate(
            flops=4 * block * n_tok * n_steps * step, bytes_accessed=2 * weights.size, transcendentals=0
        ),
        name="own_part",
    )(gated, weights)


def body(tokens, w_in, short_taps, long_filter, skip_gain, w_out):
    n_ctx, n_chips, n_cores = (lax.axis_size(axis) for axis in ("ctx", "chip", "core"))
    tok_len, width = tokens.shape
    block = w_in.shape[2]
    group_size = width // long_filter.shape[1]
    stretch = block // n_ctx
    span = min(stretch, group_size)
    piece = tok_len // n_chips

    weights = w_in.transpose(1, 0, 2)
    part = block // 32 * 11
    sent, shared = mix(group_size, tokens, short_taps, weights, long_filter, w_out, part, n_ctx)
    mine = swapped(shared, "chip")
    theirs = swapped(mine, "ctx")
    payload = lax.all_to_all(sent, "ctx", 0, 0, tiled=True)

    near, far, ends, direct = make_query(
        group_size, tokens, short_taps, weights, w_out, block - 2 * part, sent, n_chips
    )
    far, direct = swapped(far, "chip"), swapped(direct, "chip")
    before = passed_along(ends, "ctx", 1)

    gain = lax.dynamic_slice_in_dim(skip_gain, fft_index() * block + lax.axis_index("ctx") * stretch, stretch, 0)
    conv = convolve(group_size, span, stretch, payload, short_taps, arrived(gain[:, None], mine, ends), n_chips)
    fix = make_fix(group_size, before, arrived(ends, conv), short_taps)
    conv = lax.all_to_all(conv.reshape(n_chips * n_ctx, stretch, piece), ("chip", "ctx"), 0, 0, tiled=True)
    conv = conv.reshape(n_chips, block, piece)

    fixes = (arrived(fix, theirs, direct, far), swapped(fix, "chip"))
    other, staged, gated = other_part((near, far), fixes, conv, (w_out, mine, theirs, direct))
    other = swapped(other, "core")
    return (own_part(gated, staged) + other.astype(jnp.float32)).astype(jnp.bfloat16)


def solution(mesh):
    n_ctx, n_fft = (mesh.shape[axis] for axis in ("ctx", "fft"))
    split = jax.sharding.Mesh(mesh.devices.reshape(n_ctx, n_fft // 2, 2), ("ctx", "chip", "core"))
    fft = ("chip", "core")
    return jax.shard_map(
        body,
        mesh=split,
        in_specs=(P("ctx", None), P(None, None, fft), P(), P("ctx", None), P(), P(fft, None)),
        out_specs=P(("ctx",) + fft, None),
        check_vma=False,
    )
```

```python
import functools

import jax
import jax.numpy as jnp
from jax import lax
from jax.experimental import pallas as pl
from jax.experimental.pallas import tpu as pltpu
from jax.sharding import PartitionSpec as P

MIB = 1 << 20
LANES = 128
RIM = 16
LAG = 256
ARRIVED_FLOPS = 10**11
ARRIVED_VMEM = 2 * MIB
OUTPUT_VMEM = 32 * MIB
CONVOLVE_FLOPS = 10**10


def fft_index():
    return lax.axis_index("chip") * lax.axis_size("core") + lax.axis_index("core")


def passed_along(block, axis, distance):
    devices = range(lax.axis_size(axis))
    route = [(i - distance, i) for i in devices if i - distance in devices]
    return lax.ppermute(block, axis, route)


def swapped(block, axis):
    return lax.ppermute(block, axis, [(i, i ^ 1) for i in range(lax.axis_size(axis))])


def spread_taps(taps, group0, group_size):
    n_taps, n_groups = taps.shape
    rows = jnp.concatenate([taps, jnp.zeros((8 - n_taps, n_groups), jnp.float32)], axis=0)
    index = group0 + lax.broadcasted_iota(jnp.int32, (8, LANES), 1) // group_size
    return jnp.take_along_axis(rows, index, axis=1, mode="promise_in_bounds")


def filtered(coef, rows_of, n_taps):
    feat = None
    for j in range(n_taps):
        term = coef[j : j + 1, :] * rows_of(j)
        feat = term if feat is None else feat + term
    return feat.astype(jnp.bfloat16).astype(jnp.float32)


def mix_kernel(group_size, tokens, taps, weights, filt, w_out, out, shared, ext, wbuf, proj, lag, turned_lag, cut, sems):
    n_tok = tokens.shape[0]
    n_ctx = out.shape[0]
    stretch = out.shape[1] - 8
    _, n_blocks, _, width = wbuf.shape
    n_taps, n_groups = taps.shape[0], taps.shape[1] // 3
    block = n_blocks * width
    group0 = fft_index() * (block // group_size)
    main = pltpu.make_async_copy(tokens, ext, sems.at[0])
    lag_load = pltpu.make_async_copy(filt, lag, sems.at[1])
    loads = [
        pltpu.make_async_copy(weights.at[k + 1, :, pl.ds(blk * width, width)], wbuf.at[k, blk], sems.at[2 + blk * 2 + k])
        for blk in range(n_blocks)
        for k in range(2)
    ]
    lag_load.start()
    main.start()
    for load in loads:
        load.start()
    tiles = block // LANES
    for k in range(2):
        for tile in range(tiles):
            proj[k, tile, 0:RIM, :] = jnp.zeros((RIM, LANES), jnp.float32)
    coefs = [
        [
            spread_taps(taps[:, s * n_groups : (s + 1) * n_groups], group0 + tile * (LANES // group_size), group_size)
            for tile in range(tiles)
        ]
        for s in (1, 2)
    ]
    lag_load.wait()
    for at in range(0, n_tok, LANES):
        turned_lag[:, at : at + LANES] = lag[at : at + LANES, :].T
    per_lag = n_tok // (2 * LANES)
    spans = max(1, stretch // group_size)
    for dest in range(n_ctx):
        rows = []
        for g in range(spans):
            row = turned_lag[pl.ds(group0 + dest * stretch // group_size + g, 1), :]
            rows += [row[:, h * 2 * LANES : (h + 1) * 2 * LANES] for h in range(per_lag)]
        if len(rows) < 8:
            rows.append(jnp.zeros((8 - len(rows), 2 * LANES), jnp.float32))
        out[dest, stretch:, 2 * LANES :] = jnp.concatenate(rows, axis=0).astype(jnp.bfloat16)
    chunk = min(128, n_tok)
    per_block = width // LANES

    def multiply(blk):
        for k in range(2):
            full = jnp.dot(ext[...], wbuf[k, blk], preferred_element_type=jnp.float32)
            full = full.astype(jnp.bfloat16).astype(jnp.float32)
            for t in range(per_block):
                proj[k, blk * per_block + t, RIM:, :] = full[:, t * LANES : (t + 1) * LANES]

    def finish(blk):
        for tile in range(blk * per_block, (blk + 1) * per_block):
            for row in range(0, n_tok, chunk):
                key, value = [
                    filtered(coefs[k][tile], lambda j: proj[k, tile, RIM + row - j : RIM + row - j + chunk, :], n_taps)
                    for k in range(2)
                ]
                flipped = (key * value).T.astype(jnp.bfloat16)
                for c in range(0, LANES, stretch):
                    out[(tile * LANES + c) // stretch, 0:stretch, row : row + chunk] = flipped[c : c + stretch, :]

    part = shared.shape[0]
    parity = lax.axis_index("ctx") % 2
    fetch = pltpu.make_async_copy(
        w_out.at[pl.ds(pl.multiple_of(parity * part, part), part)], cut, sems.at[2 + 2 * n_blocks]
    )
    store = pltpu.make_async_copy(cut, shared, sems.at[3 + 2 * n_blocks])
    main.wait()
    for blk in range(n_blocks):
        for load in loads[2 * blk : 2 * blk + 2]:
            load.wait()
        if blk == n_blocks - 1:
            fetch.start()
        multiply(blk)
        if blk:
            finish(blk - 1)
    fetch.wait()
    store.start()
    finish(n_blocks - 1)
    low = lax.broadcasted_iota(jnp.int32, (8, LANES), 1) < LANES // 2
    for dest in range(n_ctx):
        tile, lane = divmod(dest * stretch, LANES)
        for k in range(2):
            head = proj[k, tile, RIM : RIM + 8, :]
            tail = proj[k, tile, RIM + n_tok - 8 :, :]
            if lane:
                head = pltpu.roll(head, LANES - lane, 1)
            if lane != LANES // 2:
                tail = pltpu.roll(tail, (LANES // 2 - lane) % LANES, 1)
            out[dest, stretch:, k * LANES : (k + 1) * LANES] = jnp.where(low, head, tail).astype(jnp.bfloat16)
    store.wait()


def mix(group_size, tokens, taps, weights, filt, w_out, part, n_ctx):
    n_tok, depth = tokens.shape
    block = weights.shape[2]
    width = min(256, block)
    stretch = block // n_ctx
    shared = (part, w_out.shape[1])
    hbm = pl.BlockSpec(memory_space=pltpu.HBM)
    vmem = pl.BlockSpec(memory_space=pltpu.VMEM)
    return pl.pallas_call(
        functools.partial(mix_kernel, group_size),
        out_shape=[jax.ShapeDtypeStruct(shape, jnp.bfloat16) for shape in ((n_ctx, stretch + 8, n_tok), shared)],
        in_specs=[hbm, vmem, hbm, hbm, hbm],
        out_specs=[vmem, hbm],
        scratch_shapes=[
            pltpu.VMEM((n_tok, depth), jnp.bfloat16),
            pltpu.VMEM((2, block // width, depth, width), jnp.bfloat16),
            pltpu.VMEM((2, block // LANES, RIM + n_tok, LANES), jnp.float32),
            pltpu.VMEM(filt.shape, jnp.float32),
            pltpu.VMEM(filt.shape[::-1], jnp.float32),
            pltpu.VMEM(shared, jnp.bfloat16),
            pltpu.SemaphoreType.DMA((4 + 2 * (block // width),)),
        ],
        compiler_params=pltpu.CompilerParams(vmem_limit_bytes=56 * MIB),
        cost_estimate=pl.CostEstimate(
            flops=4 * n_tok * depth * block, bytes_accessed=2 * (n_tok * depth + 2 * depth * block), transcendentals=0
        ),
        name="mix",
    )(tokens, taps, weights, filt, w_out)


def query_kernel(group_size, tokens, taps, weights, w_out, after, mine, other, ends, direct, pieces, ext, wbuf, proj, cut, sems):
    n_tok = tokens.shape[0]
    block = wbuf.shape[1]
    n_taps, n_groups = taps.shape[0], taps.shape[1] // 3
    piece = pieces.shape[2]
    group0 = fft_index() * (block // group_size)
    main = pltpu.make_async_copy(tokens, ext, sems.at[0])
    load = pltpu.make_async_copy(weights.at[0], wbuf, sems.at[1])
    rest = direct.shape[0]
    fetch = pltpu.make_async_copy(w_out.at[pl.ds(w_out.shape[0] - rest, rest)], cut, sems.at[2])
    store = pltpu.make_async_copy(cut, direct, sems.at[3])
    main.start()
    load.start()
    fetch.start()
    tiles = block // LANES
    for tile in range(tiles):
        proj[tile, 0:RIM, :] = jnp.zeros((RIM, LANES), jnp.float32)
    main.wait()
    load.wait()
    fetch.wait()
    store.start()
    full = jnp.dot(ext[...], wbuf[...], preferred_element_type=jnp.float32)
    full = full.astype(jnp.bfloat16).astype(jnp.float32)
    for tile in range(tiles):
        proj[tile, RIM:, :] = full[:, tile * LANES : (tile + 1) * LANES]
    for tile in range(tiles):
        lanes = slice(tile * LANES, (tile + 1) * LANES)
        coef = spread_taps(taps[:, :n_groups], group0 + tile * (LANES // group_size), group_size)
        both = jnp.concatenate([proj[tile, RIM + n_tok - 8 :, :], proj[tile, RIM : RIM + 8, :]], axis=0)
        ends[:, lanes] = both.astype(jnp.bfloat16)
        for row in range(0, n_tok, LANES):
            feat = filtered(coef, lambda j: proj[tile, RIM + row - j : RIM + row - j + LANES, :], n_taps)
            at = row % piece
            pieces[row // piece, lanes, at : at + LANES] = feat.T.astype(jnp.bfloat16)
    chip = lax.axis_index("chip")
    mine[...] = pieces[chip]
    other[...] = pieces[chip ^ 1]
    store.wait()


def make_query(group_size, tokens, taps, weights, w_out, rest, after, n_chips):
    n_tok, depth = tokens.shape
    block = weights.shape[2]
    hbm = pl.BlockSpec(memory_space=pltpu.HBM)
    vmem = pl.BlockSpec(memory_space=pltpu.VMEM)
    piece = (block, n_tok // n_chips)
    direct = (rest, w_out.shape[1])
    return pl.pallas_call(
        functools.partial(query_kernel, group_size),
        out_shape=[jax.ShapeDtypeStruct(shape, jnp.bfloat16) for shape in (piece, piece, (16, block), direct)],
        in_specs=[hbm, vmem, hbm, hbm, hbm],
        out_specs=[vmem] * 3 + [hbm],
        scratch_shapes=[
            pltpu.VMEM((n_chips,) + piece, jnp.bfloat16),
            pltpu.VMEM((n_tok, depth), jnp.bfloat16),
            pltpu.VMEM((depth, block), jnp.bfloat16),
            pltpu.VMEM((block // LANES, RIM + n_tok, LANES), jnp.float32),
            pltpu.VMEM(direct, jnp.bfloat16),
            pltpu.SemaphoreType.DMA((4,)),
        ],
        compiler_params=pltpu.CompilerParams(vmem_limit_bytes=56 * MIB),
        cost_estimate=pl.CostEstimate(
            flops=2 * n_tok * depth * block, bytes_accessed=2 * (n_tok * depth + depth * block), transcendentals=0
        ),
        name="query",
    )(tokens, taps, weights, w_out, after)


def fix_kernel(group_size, before, ends, taps, out):
    n_taps, n_groups = taps.shape[0], taps.shape[1] // 3
    block = out.shape[1]
    group0 = fft_index() * (block // group_size)
    for tile in range(block // LANES):
        lanes = slice(tile * LANES, (tile + 1) * LANES)
        coef = spread_taps(taps[:, :n_groups], group0 + tile * (LANES // group_size), group_size)
        both = jnp.concatenate(
            [before[:, lanes].astype(jnp.float32)[:8], ends[:, lanes].astype(jnp.float32)[8:]], axis=0
        )
        feat = filtered(coef, lambda j: both[8 - j : 16 - j, :], n_taps)
        out[:, lanes] = jnp.concatenate([feat, jnp.zeros((8, LANES), jnp.float32)], axis=0).astype(jnp.bfloat16)


def make_fix(group_size, before, ends, taps):
    vmem = pl.BlockSpec(memory_space=pltpu.VMEM)
    return pl.pallas_call(
        functools.partial(fix_kernel, group_size),
        out_shape=jax.ShapeDtypeStruct(ends.shape, jnp.bfloat16),
        in_specs=[vmem] * 3,
        out_specs=vmem,
        compiler_params=pltpu.CompilerParams(vmem_limit_bytes=16 * MIB),
        cost_estimate=pl.CostEstimate(flops=10**6, bytes_accessed=10**5, transcendentals=0),
        name="fix",
    )(before, ends, taps)


def convolve_kernel(group_size, sizes, payload, taps, gain, out, lags, fixed, lagrow, held, total):
    stretch, span, rows = sizes
    n_src, _, cols = payload.shape
    n_ctx, n_chips, _, piece = out.shape
    n_taps, n_groups = taps.shape[0], taps.shape[1] // 3
    n_blocks = n_src * cols // LAG
    per_src = cols // LAG
    pieces = LAG // piece
    size = n_blocks * rows
    length = n_src * cols
    static = n_blocks <= 16
    lead = 0 if static else size

    group0 = (fft_index() * stretch * n_ctx + lax.axis_index("ctx") * stretch) // group_size
    coefs = [
        spread_taps(taps[:, s * n_groups : (s + 1) * n_groups], group0, group_size) for s in (1, 2)
    ]
    ends = [[payload[s, stretch:, k * LANES : (k + 1) * LANES].astype(jnp.float32) for k in range(2)] for s in range(n_src)]
    first = []
    for s in range(n_src):
        made = None
        for k in range(2):
            before = pltpu.roll(ends[s - 1][k], LANES // 2, 1) if s else jnp.zeros((8, LANES), jnp.float32)
            both = jnp.concatenate([before, ends[s][k]], axis=0)
            feat = filtered(coefs[k], lambda j: both[8 - j : 16 - j, :], n_taps)
            made = feat if made is None else made * feat
        first.append(made)
    for s in range(0, n_src, 16):
        some = first[s : s + 16]
        if len(some) < 16:
            some = some + [jnp.zeros(((16 - len(some)) * 8, LANES), jnp.float32)]
        fixed[:, s * 8 : s * 8 + LANES] = jnp.concatenate(some, axis=0).T
    lane = lax.broadcasted_iota(jnp.int32, (span, LANES), 1)

    per_lag = cols // (2 * LANES)
    for s in range(n_src):
        piece_rows = payload[s, stretch:, 2 * LANES :].astype(jnp.float32)
        for g in range(stretch // span):
            for h in range(per_lag):
                at = s * cols + h * 2 * LANES
                lagrow[g : g + 1, at : at + 2 * LANES] = piece_rows[g * per_lag + h : g * per_lag + h + 1, :]
    zeros = jnp.zeros((1, LANES), jnp.float32)

    def lag_block(g, d):
        if static:
            at = d * LAG
            return jnp.concatenate([lags[g, :, at + LANES : at + LANES + LAG], lags[g, :, at : at + LAG]], axis=0)
        at = pl.multiple_of(d * LAG, LAG)
        near = lags[g, :, pl.ds(pl.multiple_of(at + LANES, LANES), LAG)]
        return jnp.concatenate([near, lags[g, :, pl.ds(at, LAG)]], axis=0)

    n_spans = stretch // span

    def prepare(g):
        row = jnp.concatenate([zeros, lagrow[g : g + 1, :], zeros], axis=1)
        wide = jnp.broadcast_to(row, (LANES, length + 2 * LANES))
        turned = pltpu.roll(wide, 0, 1, stride=1, stride_axis=0)
        lags[g] = turned[:, : length + LANES].astype(jnp.bfloat16)
        chans = slice(g * span, (g + 1) * span)
        if rows != span or lead:
            held[g] = jnp.zeros(held.shape[1:], held.dtype)
        for i in range(n_blocks):
            s = i // per_src
            part = payload[s, chans, (i % per_src) * LAG : (i % per_src + 1) * LAG]
            at = lead + i * rows
            held[g, at : at + span, :] = part
            if i % per_src == 0:
                patch = fixed[chans, s // 16 * LANES : (s // 16 + 1) * LANES]
                if s % 16:
                    patch = pltpu.roll(patch, LANES - s % 16 * 8, 1)
                patched = jnp.where(lane < 8, patch, part[:, :LANES].astype(jnp.float32))
                held[g, at : at + span, :LANES] = patched.astype(jnp.bfloat16)

    def multiply(g):
        if static:
            total[g] = jnp.dot(held[g], lag_block(g, 0), preferred_element_type=jnp.float32)
            for d in range(1, n_blocks):
                part = jnp.dot(held[g, : size - d * rows, :], lag_block(g, d), preferred_element_type=jnp.float32)
                total[g, d * rows :, :] += part
        else:
            total[g] = jnp.zeros(total.shape[1:], total.dtype)

            @pl.loop(0, n_blocks)
            def _(d):
                shifted = held[g, pl.ds(pl.multiple_of(size - d * rows, rows), size), :]
                total[g] += jnp.dot(shifted, lag_block(g, d), preferred_element_type=jnp.float32)

    def store(g):
        chans = slice(g * span, (g + 1) * span)
        for i in range(n_blocks):
            at = lead + i * rows
            direct = gain[chans, :] * held[g, at : at + span, :].astype(jnp.float32)
            both = (total[g, i * rows : i * rows + span, :] + direct).astype(jnp.bfloat16)
            for h in range(pieces):
                at = i * pieces + h
                out[at // n_chips, at % n_chips, chans, :] = both[:, h * piece : (h + 1) * piece]

    prepare(0)
    for g in range(n_spans):
        if g + 1 < n_spans:
            prepare(g + 1)
        multiply(g)
        store(g)


def convolve(group_size, span, stretch, payload, taps, gain, n_chips):
    n_src, _, cols = payload.shape
    n_blocks = n_src * cols // LAG
    rows = max(span, 16)
    size = n_blocks * rows
    length = n_src * cols
    spans = stretch // span
    held = size if n_blocks <= 16 else 2 * size
    vmem = pl.BlockSpec(memory_space=pltpu.VMEM)
    return pl.pallas_call(
        functools.partial(convolve_kernel, group_size, (stretch, span, rows)),
        out_shape=jax.ShapeDtypeStruct((n_src, n_chips, stretch, cols // n_chips), jnp.bfloat16),
        in_specs=[vmem, vmem, vmem],
        out_specs=vmem,
        scratch_shapes=[
            pltpu.VMEM((spans, LANES, length + LANES), jnp.bfloat16),
            pltpu.VMEM((LANES, -(-n_src // 16) * LANES), jnp.float32),
            pltpu.VMEM((8, length), jnp.float32),
            pltpu.VMEM((spans, held, LAG), jnp.bfloat16),
            pltpu.VMEM((spans, size, LAG), jnp.float32),
        ],
        compiler_params=pltpu.CompilerParams(vmem_limit_bytes=48 * MIB),
        cost_estimate=pl.CostEstimate(
            flops=CONVOLVE_FLOPS, bytes_accessed=4 * payload.size, transcendentals=0
        ),
        name="convolve",
    )(payload, taps, gain)


def arrived_kernel(kept, *refs):
    refs[-1][...] = kept[...]


def arrived(kept, *blocks):
    vmem = pl.BlockSpec(memory_space=pltpu.VMEM)
    return pl.pallas_call(
        arrived_kernel,
        out_shape=jax.ShapeDtypeStruct(kept.shape, kept.dtype),
        in_specs=[vmem] + [pl.BlockSpec(memory_space=pltpu.HBM)] * len(blocks),
        out_specs=vmem,
        compiler_params=pltpu.CompilerParams(vmem_limit_bytes=ARRIVED_VMEM),
        cost_estimate=pl.CostEstimate(flops=ARRIVED_FLOPS, bytes_accessed=0, transcendentals=0),
        name="arrived",
    )(kept, *blocks)


def other_kernel(q_near, q_far, fix_near, fix_far, conv, w_near, mine, theirs, direct, other, wbuf, gated, sems):
    n_tok, width = other.shape
    block = w_near.shape[0]
    part = mine.shape[0]
    chip, core = lax.axis_index("chip"), lax.axis_index("core")
    parity = lax.axis_index("ctx") % 2
    loads = []
    for n in range(wbuf.shape[0]):
        columns = pl.ds(n * wbuf.shape[3], wbuf.shape[3])
        pairs = [(w_near, wbuf.at[n, 0])]
        for k, w in enumerate((mine, theirs)):
            pairs.append((w, wbuf.at[n, 1, pl.ds(pl.multiple_of((parity ^ k) * part, part), part)]))
        pairs.append((direct, wbuf.at[n, 1, pl.ds(2 * part, block - 2 * part)]))
        loads.append(
            [pltpu.make_async_copy(w.at[:, columns], to, sems.at[4 * n + i]) for i, (w, to) in enumerate(pairs)]
        )
    for step in loads:
        for load in step:
            load.start()
    early = lax.broadcasted_iota(jnp.int32, (block, LANES), 1) < 8

    def channels_first(fix):
        rows = jnp.concatenate([fix[...].astype(jnp.float32), jnp.zeros((LANES - 16, block), jnp.float32)], axis=0)
        return jnp.concatenate([rows[:, at : at + LANES].T for at in range(0, block, LANES)], axis=0)

    fixes = [channels_first(fix) for fix in (fix_near, fix_far)]

    def gate(k, half):
        query = (q_near, q_far)[k]
        pieces = []
        for t in range(0, n_tok, LANES):
            at = pl.ds(pl.multiple_of((core ^ half) * n_tok + t, LANES), LANES)
            values = query[:, at].astype(jnp.float32)
            if t == 0:
                first = jnp.logical_and(early, jnp.logical_and(chip == 0, core == half))
                values = jnp.where(first, fixes[k], values)
            source = jnp.concatenate([conv[s, chip ^ k, :, at] for s in range(conv.shape[0])], axis=0)
            product = values * source.astype(jnp.float32)
            pieces.append(product.T.astype(jnp.bfloat16))
        return pieces[0] if len(pieces) == 1 else jnp.concatenate(pieces, axis=0)

    theirs_gated = [gate(k, 1) for k in range(2)]
    for k in range(2):
        gated[k] = gate(k, 0)
    for n, step in enumerate(loads):
        for load in step:
            load.wait()
        acc = jnp.dot(theirs_gated[0], wbuf[n, 0], preferred_element_type=jnp.float32)
        acc += jnp.dot(theirs_gated[1], wbuf[n, 1], preferred_element_type=jnp.float32)
        other[:, n * wbuf.shape[3] : (n + 1) * wbuf.shape[3]] = acc.astype(other.dtype)


def other_part(query, fixes, conv, weights):
    block, n_tok = query[0].shape
    n_tok //= 2
    width = weights[0].shape[1]
    step = width // 2
    vmem = pl.BlockSpec(memory_space=pltpu.VMEM)
    hbm = pl.BlockSpec(memory_space=pltpu.HBM)
    shapes = (n_tok, width), (width // step, 2, block, step), (2, n_tok, block)
    return pl.pallas_call(
        other_kernel,
        out_shape=[jax.ShapeDtypeStruct(shape, jnp.bfloat16) for shape in shapes],
        in_specs=[vmem] * 5 + [hbm] * 4,
        out_specs=[vmem] * 3,
        scratch_shapes=[pltpu.SemaphoreType.DMA((4 * (width // step),))],
        compiler_params=pltpu.CompilerParams(vmem_limit_bytes=OUTPUT_VMEM),
        cost_estimate=pl.CostEstimate(
            flops=4 * block * n_tok * width, bytes_accessed=4 * block * width, transcendentals=0
        ),
        name="other_part",
    )(*query, *fixes, conv, *weights)


def own_kernel(gated, weights, out):
    step = weights.shape[3]
    for n in range(weights.shape[0]):
        acc = jnp.dot(gated[0], weights[n, 0], preferred_element_type=jnp.float32)
        acc += jnp.dot(gated[1], weights[n, 1], preferred_element_type=jnp.float32)
        out[:, n * step : (n + 1) * step] = acc


def own_part(gated, weights):
    n_steps, _, block, step = weights.shape
    n_tok = gated.shape[1]
    vmem = pl.BlockSpec(memory_space=pltpu.VMEM)
    return pl.pallas_call(
        own_kernel,
        out_shape=jax.ShapeDtypeStruct((n_tok, n_steps * step), jnp.float32),
        in_specs=[vmem] * 2,
        out_specs=vmem,
        compiler_params=pltpu.CompilerParams(vmem_limit_bytes=24 * MIB),
        cost_estimate=pl.CostEstimate(
            flops=4 * block * n_tok * n_steps * step, bytes_accessed=2 * weights.size, transcendentals=0
        ),
        name="own_part",
    )(gated, weights)


def body(tokens, w_in, short_taps, long_filter, skip_gain, w_out):
    n_ctx, n_chips, n_cores = (lax.axis_size(axis) for axis in ("ctx", "chip", "core"))
    tok_len, width = tokens.shape
    block = w_in.shape[2]
    group_size = width // long_filter.shape[1]
    stretch = block // n_ctx
    span = min(stretch, group_size)
    piece = tok_len // n_chips

    weights = w_in.transpose(1, 0, 2)
    part = block // 32 * 11
    sent, shared = mix(group_size, tokens, short_taps, weights, long_filter, w_out, part, n_ctx)
    mine = swapped(shared, "chip")
    theirs = swapped(mine, "ctx")
    payload = lax.all_to_all(sent, "ctx", 0, 0, tiled=True)

    near, far, ends, direct = make_query(
        group_size, tokens, short_taps, weights, w_out, block - 2 * part, sent, n_chips
    )
    far, direct = swapped(far, "chip"), swapped(direct, "chip")
    before = passed_along(ends, "ctx", 1)

    gain = lax.dynamic_slice_in_dim(skip_gain, fft_index() * block + lax.axis_index("ctx") * stretch, stretch, 0)
    conv = convolve(group_size, span, stretch, payload, short_taps, arrived(gain[:, None], mine, ends), n_chips)
    fix = make_fix(group_size, before, arrived(ends, conv), short_taps)
    conv = lax.all_to_all(conv.reshape(n_ctx * n_chips, stretch, piece), ("ctx", "chip"), 0, 0, tiled=True)
    conv = conv.reshape(n_ctx, n_chips, stretch, piece)

    fixes = (arrived(fix, theirs, direct, far), swapped(fix, "chip"))
    other, staged, gated = other_part((near, far), fixes, conv, (w_out, mine, theirs, direct))
    other = swapped(other, "core")
    return (own_part(gated, staged) + other.astype(jnp.float32)).astype(jnp.bfloat16)


def solution(mesh):
    n_ctx, n_fft = (mesh.shape[axis] for axis in ("ctx", "fft"))
    split = jax.sharding.Mesh(mesh.devices.reshape(n_ctx, n_fft // 2, 2), ("ctx", "chip", "core"))
    fft = ("chip", "core")
    return jax.shard_map(
        body,
        mesh=split,
        in_specs=(P("ctx", None), P(None, None, fft), P(), P("ctx", None), P(), P(fft, None)),
        out_specs=P(("ctx",) + fft, None),
        check_vma=False,
    )
```
